32 devices in a mesh: gx: 8 (over y, x, core), gy: 4 (over z).
Axes of the slice: x: 2, y: 2, z: 4, core: 2. Of those that a mesh axis runs over, the one named last changes fastest.
Arguments:
- velocity: float32 [2, 10, 768, 1536], P(None, None, 'gx', 'gy'), may hold values from -6 to 6
- viscosity: float32 [10, 768, 1536], P(None, 'gx', 'gy'), may hold values from 0.05 to 0.8
- friction: float32 [768, 1536], P('gx', 'gy'), may hold values from 0.1 to 2
- ice_mask: int32 [8, 4], P('gx', 'gy'), may hold values from 0 to 1, as said below
- obs_tiles: float32 [8, 4, 8, 4, 4, 3, 128], P('gx', 'gy'), as said below
- obs_cell: int32 [8, 4, 8, 4, 4], P('gx', 'gy'), may hold values from 0 to 287, as said below
- obs_count: int32 [8, 4, 8, 4], P('gx', 'gy'), may hold values from 0 to 4, as said below
Outputs:
- adjoint: float32 [2, 10, 768, 1536], P(None, None, 'gx', 'gy')
- friction_gradient: float32 [768, 1536], P('gx', 'gy')
The draws below stay inside these ranges and needn't reach their ends.
Inputs may be any that keep to these rules, and one draw needn't show every extreme that they name: `ice_mask`: some block is ice-covered in every draw. `obs_count`: zero for every owner block whose ice_mask is 0; in every draw some owner block receives 4 live tiles from every sending block. `obs_cell`: slots at or beyond the live count also hold anchors in range. `obs_tiles`: channel 2 holds weights between 0.3 and 3.
All inputs are finite; a program needn't handle non-finite values.
Results may differ from the reference program's by a relative error of at most 0.00002.
Values sent between devices are 32-bit elements; how exact they have to be, the bound alone decides.
No kernel may reach another device: no remote copies, remote signals or barrier semaphores. Data moves between devices by JAX's collectives and lax.ppermute only.
A program may use at most 128 MiB of HBM per device.

```python
import math
import jax
import jax.numpy as jnp

CX = 96
CY = 384
LAYERS = 10
SWEEPS = 3
TILE = 128
CAP = 4
BLOCKS_X = 8
BLOCKS_Y = 4
NX = 768
NY = 1536
NB = 3


def ice_and_full(key):
    base = jax.random.fold_in(key, 11)
    first_key, second_key = jax.random.split(base)
    covered = (jax.random.randint(first_key, (BLOCKS_X * BLOCKS_Y,), 0, 4) < 3).astype(jnp.int32)
    full_owner = jax.random.randint(second_key, (), 0, BLOCKS_X * BLOCKS_Y)
    covered = covered.at[full_owner].set(1)
    return (covered.reshape(BLOCKS_X, BLOCKS_Y), full_owner)


def draw_ice_mask(key, part):
    covered, full_owner = ice_and_full(key)
    return covered


def draw_obs_count(key, part):
    covered, full_owner = ice_and_full(key)
    count_key = jax.random.fold_in(key, 12)
    counts = jax.random.randint(count_key, (BLOCKS_X, BLOCKS_Y, BLOCKS_X, BLOCKS_Y), 1, CAP + 1)
    counts = counts * covered[None, None, :, :]
    counts = counts.reshape(BLOCKS_X, BLOCKS_Y, BLOCKS_X * BLOCKS_Y).at[:, :, full_owner].set(CAP)
    return counts.reshape(BLOCKS_X, BLOCKS_Y, BLOCKS_X, BLOCKS_Y).astype(jnp.int32)


def draw_obs_cell(key, part):
    cell_key = jax.random.fold_in(key, 13)
    cells = jax.random.randint(cell_key, (BLOCKS_X * BLOCKS_Y * BLOCKS_X * BLOCKS_Y * CAP,), 0, CX * NB)
    cells = cells.at[0].set(CX * NB - 1).at[1].set(0)
    return cells.reshape(BLOCKS_X, BLOCKS_Y, BLOCKS_X, BLOCKS_Y, CAP).astype(jnp.int32)


def draw_obs_tiles(key, part):
    tile_key = jax.random.fold_in(key, 14)
    u_key, v_key, w_key = jax.random.split(tile_key, 3)
    shape_one = (BLOCKS_X, BLOCKS_Y, BLOCKS_X, BLOCKS_Y, CAP, TILE)
    u_obs = jax.random.normal(u_key, shape_one, jnp.float32)
    v_obs = jax.random.normal(v_key, shape_one, jnp.float32)
    weights = jnp.exp(jax.random.uniform(w_key, shape_one, jnp.float32, jnp.log(0.3), jnp.log(3.0)))
    return jnp.stack([u_obs, v_obs, weights], axis=-2).astype(jnp.float32)


def steps_of(key, dims, cuts, least, top_value):
    factor_of = 1.0
    for axis_at, shards_of in cuts:
        steps = jax.random.uniform(jax.random.fold_in(jax.random.fold_in(key, 6), axis_at), (shards_of,), jnp.float32, least / len(cuts), top_value / len(cuts))
        factor_of = factor_of * jnp.repeat(jnp.exp(steps), dims[axis_at] // shards_of).reshape((-1,) + (1,) * (len(dims) - 1 - axis_at))
    return factor_of


def centred(rng, shape, width, reach, cuts=(), held_as=jnp.bfloat16):
    drawn = jax.random.normal(rng, shape, jnp.float32) * width
    if len(cuts) > 0:
        drawn = steps_of(rng, shape, cuts, -0.22, 0.18) * drawn
    return jnp.clip(drawn, min=-reach, max=reach).astype(held_as)


def setup_inputs(seed: int = 0) -> dict:
    streams_of = jax.random.split(jax.random.key(seed), 8)
    return {
        "velocity": centred(streams_of[0], (2, LAYERS, NX, NY), 1.0, 6.0, ((2, 8), (3, 4)), jnp.float32),
        "viscosity": jnp.clip(jnp.exp(math.log(0.8) - 2.7725887 * jax.random.uniform(streams_of[1], (LAYERS, NX, NY), jnp.float32) ** steps_of(streams_of[1], (LAYERS, NX, NY), ((1, 8), (2, 4)), -0.2, 0.2)), 0.05, 0.8),
        "friction": jnp.clip(jnp.exp(math.log(2.0) - 2.9957323 * jax.random.uniform(streams_of[2], (NX, NY), jnp.float32) ** steps_of(streams_of[2], (NX, NY), ((0, 8), (1, 4)), -0.2, 0.2)), 0.1, 2.0),
        "ice_mask": draw_ice_mask(jax.random.fold_in(streams_of[7], 71), 0),
        "obs_tiles": draw_obs_tiles(jax.random.fold_in(streams_of[7], 71), 0),
        "obs_cell": draw_obs_cell(jax.random.fold_in(streams_of[7], 71), 0),
        "obs_count": draw_obs_count(jax.random.fold_in(streams_of[7], 71), 0),
    }


VERTICAL_GAIN = 2.0
RELAX_WEIGHT = 0.8


def column_factors(padded_visc, friction_field):
    center = padded_visc[:, 1:-1, 1:-1]
    west_face = 0.5 * (center + padded_visc[:, :-2, 1:-1])
    east_face = 0.5 * (center + padded_visc[:, 2:, 1:-1])
    south_face = 0.5 * (center + padded_visc[:, 1:-1, :-2])
    north_face = 0.5 * (center + padded_visc[:, 1:-1, 2:])
    upper_face = VERTICAL_GAIN * 0.5 * (center[:-1] + center[1:])
    layer_count = center.shape[0]
    diagonal = west_face + east_face + south_face + north_face
    pivots = []
    ratios = []
    for level in range(layer_count):
        entry = diagonal[level]
        if level == 0:
            entry = entry + friction_field
        if level < layer_count - 1:
            entry = entry + upper_face[level]
        if level > 0:
            entry = entry + upper_face[level - 1] + upper_face[level - 1] * ratios[level - 1]
        pivots.append(entry)
        if level < layer_count - 1:
            ratios.append(-upper_face[level] / entry)
    return (west_face, east_face, south_face, north_face, upper_face, pivots, ratios)


def relax(padded_adj, rhs_field, factors, icefield):
    west_face, east_face, south_face, north_face, upper_face, pivots, ratios = factors
    center = padded_adj[..., 1:-1, 1:-1]
    driven = rhs_field + west_face * padded_adj[..., :-2, 1:-1] + east_face * padded_adj[..., 2:, 1:-1]
    driven = driven + south_face * padded_adj[..., 1:-1, :-2] + north_face * padded_adj[..., 1:-1, 2:]
    layer_count = len(pivots)
    forward = []
    for level in range(layer_count):
        value = driven[:, level]
        if level > 0:
            value = value + upper_face[level - 1] * forward[level - 1]
        forward.append(value / pivots[level])
    solved = [forward[-1]]
    for level in range(layer_count - 2, -1, -1):
        solved.insert(0, forward[level] - ratios[level] * solved[0])
    stacked = jnp.stack(solved, axis=1)
    return icefield * ((1.0 - RELAX_WEIGHT) * center + RELAX_WEIGHT * stacked)


def reference(velocity, viscosity, friction, ice_mask, obs_tiles, obs_cell, obs_count):
    icefield = jnp.repeat(jnp.repeat(ice_mask.astype(jnp.float32), CX, axis=0), CY, axis=1)
    live_slot = (jnp.arange(CAP, dtype=jnp.int32)[None, None, None, None, :] < obs_count[..., None]).astype(jnp.float32)
    weight = obs_tiles[..., 2, :] * live_slot[..., None]
    owner_x = jnp.arange(BLOCKS_X, dtype=jnp.int32)[None, None, :, None, None]
    owner_y = jnp.arange(BLOCKS_Y, dtype=jnp.int32)[None, None, None, :, None]
    row_global = (owner_x * CX + obs_cell // NB).astype(jnp.int32)
    tile_global = (owner_y * NB + obs_cell % NB).astype(jnp.int32)
    surface = velocity[:, LAYERS - 1].reshape(2, NX, NY // TILE, TILE)
    sampled = surface[:, row_global, tile_global, :]
    observed = jnp.moveaxis(obs_tiles[..., :2, :], -2, 0)
    contrib = weight[None] * (sampled - observed)
    top_layer = jnp.zeros((2, NX, NY // TILE, TILE), jnp.float32).at[:, row_global, tile_global].add(contrib)
    rhs_field = jnp.zeros((2, LAYERS, NX, NY), jnp.float32).at[:, LAYERS - 1].set(top_layer.reshape(2, NX, NY))
    factors = column_factors(jnp.pad(viscosity, ((0, 0), (1, 1), (1, 1))), friction)
    adjoint = jnp.zeros((2, LAYERS, NX, NY), jnp.float32)
    for sweep_index in range(SWEEPS):
        padded = jnp.pad(adjoint, ((0, 0), (0, 0), (1, 1), (1, 1)))
        adjoint = relax(padded, rhs_field, factors, icefield)
    gradient = -icefield * (adjoint[0, 0] * velocity[0, 0] + adjoint[1, 0] * velocity[1, 0])
    return adjoint, gradient
```

```python
import functools

import jax
import jax.numpy as jnp
from jax import lax
from jax.experimental import pallas as pl
from jax.experimental.pallas import tpu as pltpu
from jax.sharding import PartitionSpec as P

VERTICAL_GAIN = 2.0
RELAX_WEIGHT = 0.8

TOP = 16
FACES = 6


def lanes_of(shape):
    return lax.broadcasted_iota(jnp.int32, shape, len(shape) - 1)


def three_parts(value):
    high = value.astype(jnp.bfloat16)
    rest = value - high.astype(jnp.float32)
    middle = rest.astype(jnp.bfloat16)
    low = (rest - middle.astype(jnp.float32)).astype(jnp.bfloat16)
    return jnp.concatenate([high, middle, low], axis=-1)


def sum_parts(value):
    width = value.shape[-1] // 3
    return value[:, :width] + value[:, width : 2 * width] + value[:, 2 * width :]


def pick(onehot, value):
    return sum_parts(jnp.dot(onehot, three_parts(value), preferred_element_type=jnp.float32))


def spread(onehot, value):
    dims = (((0,), (0,)), ((), ()))
    return sum_parts(
        lax.dot_general(onehot, three_parts(value), dims, preferred_element_type=jnp.float32)
    )


def pack_kernel(
    owners_x, owners_y, count_ref, ice_ref, tiles_ref, cells_ref, low_ref, high_ref, low_fric, high_fric, out_ref, xlo_ref, xhi_ref
):
    layers = low_ref.shape[0]
    slots, lanes = tiles_ref.shape[2], tiles_ref.shape[3]
    lane = lanes_of((slots, lanes))
    slot = lax.broadcasted_iota(jnp.int32, (slots, lanes), 0)
    icefield = jnp.full((4, low_fric.shape[1]), ice_ref[0, 0], jnp.int32).astype(jnp.float32)
    for k in range(layers):
        xlo_ref[k] = low_ref[k, 0:4]
        xhi_ref[k] = high_ref[k, 4:8]
    xlo_ref[layers] = low_fric[0:4]
    xhi_ref[layers] = high_fric[4:8]
    xlo_ref[layers + 1] = icefield
    xhi_ref[layers + 1] = icefield
    zero = jnp.zeros((slots, lanes), jnp.float32)
    for ox in range(owners_x):
        firsts, lasts, owns = [], [], []
        for oy in range(owners_y):
            owner = ox * owners_y + oy
            u = tiles_ref[owner, 0]
            v = tiles_ref[owner, 1]
            w = jnp.where(slot < count_ref[ox, oy], tiles_ref[owner, 2], 0.0)
            cell = jnp.broadcast_to(cells_ref[oy, :, ox : ox + 1], (slots, lanes)).astype(jnp.float32)
            out_ref[owner, 0:slots] = u
            out_ref[owner, slots : 2 * slots] = v
            out_ref[owner, 2 * slots : 3 * slots] = w
            first = jnp.where(lane < 4, pltpu.roll(v, 2, 1), jnp.where(lane < 6, pltpu.roll(w, 4, 1), cell))
            firsts.append(jnp.where(lane < 2, u, first))
            last = jnp.where(
                lane >= lanes - 4,
                pltpu.roll(v, lanes - 2, 1),
                jnp.where(lane >= lanes - 6, pltpu.roll(w, lanes - 4, 1), cell),
            )
            lasts.append(jnp.where(lane >= lanes - 2, u, last))
            owns.append(cell)
        for oy in range(owners_y):
            after = firsts[oy + 1] if oy + 1 < owners_y else zero
            before = lasts[oy - 1] if oy > 0 else zero
            meta = jnp.where(lane < 16, after, jnp.where(lane >= lanes - 16, before, owns[oy]))
            out_ref[ox * owners_y + oy, 3 * slots : 4 * slots] = meta


def columns_kernel(
    ice_ref, visc_first, visc_last, fric_first, fric_last, vel_first, vel_last, before_ref, after_ref, first_ref, last_ref
):
    layers, rows, lanes = visc_first.shape
    lane = lanes_of((rows, lanes))
    lane_4 = lanes_of((4, lanes))
    icefield = jnp.full((rows, lanes), ice_ref[0, 0], jnp.int32).astype(jnp.float32)
    cols = before_ref.shape[2]
    first_ref[...] = jnp.zeros(first_ref.shape, jnp.float32)
    last_ref[...] = jnp.zeros(last_ref.shape, jnp.float32)
    first = jnp.zeros((rows, lanes), jnp.float32)
    last = jnp.zeros((rows, lanes), jnp.float32)
    edges = [jnp.zeros((4, lanes), jnp.float32) for _ in range(4)]
    for k in range(layers + 4):
        if k < layers:
            mine = (visc_first[k], visc_last[k])
        elif k == layers:
            mine = (fric_first[...], fric_last[...])
        elif k == layers + 1:
            mine = (icefield, icefield)
        else:
            mine = (vel_first[k - layers - 2, 0], vel_last[k - layers - 2, 0])
        here = (lane >= 3 * k) & (lane < 3 * k + 3)
        first = jnp.where(here, pltpu.roll(mine[0], 3 * k, 1), first)
        there = (lane >= lanes - 3 - 3 * k) & (lane < lanes - 3 * k)
        last = jnp.where(there, pltpu.roll(mine[1], (lanes - 3 * k) % lanes, 1), last)
        if k < layers + 2:
            here_4 = (lane_4 >= 3 * k) & (lane_4 < 3 * k + 3)
            there_4 = (lane_4 >= lanes - 3 - 3 * k) & (lane_4 < lanes - 3 * k)
            for n, ref in enumerate((before_ref, after_ref)):
                edges[n] = jnp.where(here_4, pltpu.roll(ref[k, :, 0:lanes], 3 * k, 1), edges[n])
                edges[n + 2] = jnp.where(
                    there_4, pltpu.roll(ref[k, :, cols - lanes : cols], (lanes - 3 * k) % lanes, 1), edges[n + 2]
                )
    first_ref[TOP : TOP + rows] = first
    last_ref[TOP : TOP + rows] = last
    first_ref[TOP - 4 : TOP] = edges[0]
    first_ref[TOP + rows : TOP + rows + 4] = edges[1]
    last_ref[TOP - 4 : TOP] = edges[2]
    last_ref[TOP + rows : TOP + rows + 4] = edges[3]


def side_tile(before, after, k):
    lanes = before.shape[-1]
    lane = lanes_of(before.shape)
    left = pltpu.roll(before, (3 * k) % lanes, 1)
    right = pltpu.roll(after, (lanes - 3 * k) % lanes, 1)
    return jnp.where(lane < 3, right, jnp.where(lane >= lanes - 3, left, 0.0))


def ring_pair(load, tile, tiles):
    here = load(tile)
    lanes = here.shape[-1]
    lane = lanes_of(here.shape)
    before = pltpu.roll(jnp.where(lane == lanes - 1, load((tile - 1) % tiles), here), 1, 1)
    after = pltpu.roll(jnp.where(lane == 0, load((tile + 1) % tiles), here), lanes - 1, 1)
    return here, before, after


def factors_kernel(
    ice_ref, visc_ref, fric_ref, xbefore_ref, xafter_ref, ybefore_ref, yafter_ref, coef_ref, field
):
    layers, rows, cols = visc_ref.shape
    tiles = field.shape[1]
    lanes = field.shape[3]
    high = rows + TOP
    icefield = jnp.full((rows, lanes), ice_ref[0, 0], jnp.int32).astype(jnp.float32)
    edge = jnp.zeros((TOP, lanes), jnp.float32)
    for k in range(layers + 2):
        for t in range(tiles - 1):
            span = slice(t * lanes, (t + 1) * lanes)
            field[k, t, 0:TOP] = edge
            field[k, t, high : high + TOP] = edge
            field[k, t, TOP - 4 : TOP] = xbefore_ref[k, :, span]
            field[k, t, high : high + 4] = xafter_ref[k, :, span]
            if k < layers:
                field[k, t, TOP:high] = visc_ref[k, :, span]
            elif k == layers:
                field[k, t, TOP:high] = fric_ref[:, span]
            else:
                field[k, t, TOP:high] = icefield
        field[k, tiles - 1] = side_tile(ybefore_ref[...], yafter_ref[...], k)

    def chunk(c, carry):
        row = 8 + 8 * c
        for t in range(tiles):
            gain = (0.5 * RELAX_WEIGHT) * field[layers + 1, t, pl.ds(row, 8)]
            up = None
            ratio = None
            for k in range(layers):
                here, south, north = ring_pair(lambda s: field[k, s, pl.ds(row, 8)], t, tiles)
                west = here + field[k, t, pl.ds(row - 1, 8)]
                east = here + field[k, t, pl.ds(row + 1, 8)]
                south = here + south
                north = here + north
                entry = 0.5 * (west + east + south + north)
                if k == 0:
                    entry = entry + field[layers, t, pl.ds(row, 8)]
                if k > 0:
                    entry = entry + (up - up * ratio)
                if k < layers - 1:
                    above = (0.5 * VERTICAL_GAIN) * (here + field[k + 1, t, pl.ds(row, 8)])
                    entry = entry + above
                inverse = jnp.where(entry > 0.0, 1.0 / entry, 0.0)
                scale = gain * inverse
                coef_ref[c, t, 0, k] = west * scale
                coef_ref[c, t, 1, k] = east * scale
                coef_ref[c, t, 2, k] = south * scale
                coef_ref[c, t, 3, k] = north * scale
                if k > 0:
                    coef_ref[c, t, 4, k] = up * inverse
                if k < layers - 1:
                    up = above
                    ratio = up * inverse
                    coef_ref[c, t, 5, k] = ratio
                else:
                    coef_ref[c, t, 4, 0] = 2.0 * scale
                    coef_ref[c, t, 5, k] = scale
        return carry

    lax.fori_loop(0, coef_ref.shape[0], chunk, 0)


def sources_kernel(slots, layers, tiles_ref, vel_ref, ybefore_ref, yafter_ref, rhs_ref, low_ref, high_ref):
    rows, cols = vel_ref.shape[2], vel_ref.shape[3]
    lanes = tiles_ref.shape[1]
    owners = tiles_ref.shape[0] // (4 * slots)
    blocks = cols // lanes

    def channel(c):
        return jnp.concatenate(
            [tiles_ref[pl.ds(c * slots + s, owners, stride=4 * slots), :] for s in range(slots)], axis=0
        )

    seen_u, seen_v, weight, meta = channel(0), channel(1), channel(2), channel(3)
    count = owners * slots
    lane = lanes_of((count, lanes))
    row = lanes_of((count, rows))

    def onehot(column, b):
        cell = jnp.broadcast_to(column.astype(jnp.int32), (count, rows))
        return (cell == row * blocks + b).astype(jnp.bfloat16)

    own = meta[:, lanes // 2 : lanes // 2 + 1]
    marks = jnp.concatenate([onehot(own, b) for b in range(blocks)], axis=1)
    surface = jnp.concatenate(
        [
            jnp.concatenate([vel_ref[c, 0, :, b * lanes : (b + 1) * lanes] for b in range(blocks)], axis=0)
            for c in range(2)
        ],
        axis=1,
    )
    sampled = pick(marks, surface)
    weights = jnp.concatenate([weight, weight], axis=1)
    terms = weights * (sampled - jnp.concatenate([seen_u, seen_v], axis=1))
    top = spread(marks, terms)
    for c in range(2):
        for b in range(blocks):
            plane = top[b * rows : (b + 1) * rows, c * lanes : (c + 1) * lanes]
            rhs_ref[c, b] = plane
            low_ref[c * (blocks + 1) + b] = plane[0:2]
            high_ref[c * (blocks + 1) + b] = plane[rows - 2 : rows]

    beside = jnp.concatenate(
        [
            side_tile(ybefore_ref[TOP : TOP + rows], yafter_ref[TOP : TOP + rows], layers + 2 + c)
            for c in range(2)
        ],
        axis=1,
    )
    mark_after = onehot(meta[:, 8:9], 0)
    mark_before = onehot(meta[:, lanes - 8 : lanes - 7], blocks - 1)
    weight_after = jnp.where(lane < 2, pltpu.roll(meta, lanes - 4, 1), 0.0)
    weight_before = jnp.where(lane >= lanes - 2, pltpu.roll(meta, 4, 1), 0.0)
    after = jnp.concatenate([meta, pltpu.roll(meta, lanes - 2, 1)], axis=1)
    before = jnp.concatenate([meta, pltpu.roll(meta, 2, 1)], axis=1)
    terms_after = jnp.concatenate([weight_after] * 2, axis=1) * (pick(mark_after, beside) - after)
    terms_before = jnp.concatenate([weight_before] * 2, axis=1) * (pick(mark_before, beside) - before)
    side = spread(mark_after, terms_after) + spread(mark_before, terms_before)
    for c in range(2):
        plane = side[:, c * lanes : (c + 1) * lanes]
        rhs_ref[c, blocks] = plane
        low_ref[c * (blocks + 1) + blocks] = plane[0:2]
        high_ref[c * (blocks + 1) + blocks] = plane[rows - 2 : rows]


def sweeps_kernel(
    ice_ref, coef_hbm, rhs_ref, before_ref, after_ref, vel_ref, adj_hbm, grad_ref, coef, rhs, one, two, three, sem_in, sem_out
):
    chunks, tiles, _, layers = coef.shape[:4]
    rows, cols = grad_ref.shape
    lanes = coef.shape[5]
    edge = jnp.zeros((8, lanes), jnp.float32)

    def load_copy(c):
        return pltpu.make_async_copy(coef_hbm.at[c], coef.at[c], sem_in.at[c])

    def store_copy(c):
        span = pl.ds(pl.multiple_of(8 * c, 8), 8)
        return pltpu.make_async_copy(three.at[:, :, span, :], adj_hbm.at[:, :, span, :], sem_out.at[c])

    def begin(c, carry):
        load_copy(c).start()
        return carry

    lax.fori_loop(0, chunks, begin, 0)
    for c in range(2):
        for t in range(tiles):
            rhs[c, t, 8:16] = edge
            rhs[c, t, 16 + rows : 24 + rows] = edge
            rhs[c, t, 14:16] = before_ref[c * tiles + t]
            rhs[c, t, 16 + rows : 18 + rows] = after_ref[c * tiles + t]
            rhs[c, t, 16 : 16 + rows] = rhs_ref[c, t]
            for k in range(layers):
                one[c, k, t, 0:8] = edge
                one[c, k, t, 24 + rows : 32 + rows] = edge
                two[c, k, t, 0:8] = edge
                two[c, k, t, 24 + rows : 32 + rows] = edge

    def first_sweep(c, carry):
        load_copy(c).wait()
        row = 8 + 8 * c
        for t in range(tiles):
            scale = coef[c, t, 4, 0]
            for n in range(2):
                value = rhs[n, t, pl.ds(row, 8)] * scale
                one[n, layers - 1, t, pl.ds(row, 8)] = value
                for k in range(layers - 2, -1, -1):
                    value = coef[c, t, 5, k] * value
                    one[n, k, t, pl.ds(row, 8)] = value
        return carry

    lax.fori_loop(0, chunks, first_sweep, 0)

    def relax(c, t, old, write):
        row = 8 + 8 * c
        centers, forward = [], []
        for n in range(2):
            centers.append([])
            forward.append([])
        for k in range(layers):
            west, east, south, north = (coef[c, t, f, k] for f in range(4))
            for n in range(2):
                here, before, after = ring_pair(lambda s: old[n, k, s, pl.ds(row, 8)], t, tiles)
                value = west * old[n, k, t, pl.ds(row - 1, 8)] + east * old[n, k, t, pl.ds(row + 1, 8)]
                value = value + (south * before + north * after)
                if k > 0:
                    value = value + coef[c, t, 4, k] * forward[n][k - 1]
                if k == layers - 1:
                    value = value + rhs[n, t, pl.ds(row, 8)] * coef[c, t, 4, 0]
                forward[n].append(value)
        for n in range(2):
            value = forward[n][layers - 1]
            for k in range(layers - 1, -1, -1):
                if k < layers - 1:
                    value = forward[n][k] + coef[c, t, 5, k] * value
                write(n, k, (1.0 - RELAX_WEIGHT) * old[n, k, t, pl.ds(row, 8)] + value)

    def second_sweep(c, carry):
        row = 8 + 8 * c
        for t in range(tiles):

            def write(n, k, value):
                two[n, k, t, pl.ds(row, 8)] = value

            relax(c, t, one, write)
        return carry

    lax.fori_loop(0, chunks, second_sweep, 0)
    icefield = jnp.full((8, lanes), ice_ref[0, 0], jnp.int32).astype(jnp.float32)

    def third_sweep(c, carry):
        row = pl.multiple_of(8 * c, 8)
        for t in range(tiles - 1):
            span = slice(t * lanes, (t + 1) * lanes)

            def write(n, k, value):
                three[n, k, pl.ds(row, 8), span] = value

            relax(c + 1, t, two, write)
            product = three[0, 0, pl.ds(row, 8), span] * vel_ref[0, 0, pl.ds(row, 8), span]
            product = product + three[1, 0, pl.ds(row, 8), span] * vel_ref[1, 0, pl.ds(row, 8), span]
            grad_ref[pl.ds(row, 8), span] = -icefield * product
        store_copy(c).start()
        return carry

    lax.fori_loop(0, chunks - 2, third_sweep, 0)

    def finish(c, carry):
        store_copy(c).wait()
        return carry

    lax.fori_loop(0, chunks - 2, finish, 0)


def whole(space=pltpu.VMEM):
    return pl.BlockSpec(memory_space=space)


def per_device(velocity, viscosity, friction, ice_mask, obs_tiles, obs_cell, obs_count):
    layers, rows, cols = viscosity.shape
    owners_x, owners_y, slots, channels, lanes = obs_tiles.shape[2:]
    blocks = cols // lanes
    tiles = blocks + 1
    owners = owners_x * owners_y
    chunks = rows // 8 + 2
    tall = rows + 2 * TOP
    f32 = jnp.float32

    def shift(value, axis, step):
        size = lax.axis_size(axis)
        pairs = [(i, i + step) for i in range(size) if 0 <= i + step < size]
        return lax.ppermute(value, axis, pairs)

    tiles_in = jnp.transpose(obs_tiles.reshape(owners, slots, channels, lanes), (0, 2, 1, 3))
    cells_in = jnp.transpose(obs_cell[0, 0], (1, 2, 0))
    counts_in = obs_count[0, 0]

    def part(shape, index):
        return pl.BlockSpec(shape, lambda i: index)

    side = jax.ShapeDtypeStruct((layers + 2, 4, cols), f32)
    packed, xlow, xhigh = pl.pallas_call(
        functools.partial(pack_kernel, owners_x, owners_y),
        grid=(1,),
        out_shape=(jax.ShapeDtypeStruct((owners, 4 * slots, lanes), f32), side, side),
        in_specs=[
            whole(pltpu.SMEM),
            whole(pltpu.SMEM),
            whole(),
            whole(),
            part((layers, 8, cols), (0, 0, 0)),
            part((layers, 8, cols), (0, rows // 8 - 1, 0)),
            part((8, cols), (0, 0)),
            part((8, cols), (rows // 8 - 1, 0)),
        ],
        out_specs=(whole(), whole(), whole()),
        name="pack",
    )(counts_in, ice_mask, tiles_in, cells_in, viscosity, viscosity, friction, friction)
    arrived = lax.all_to_all(packed, ("gx", "gy"), split_axis=0, concat_axis=0, tiled=True)
    xbefore = shift(xhigh, "gx", 1)
    xafter = shift(xlow, "gx", -1)

    plane = jax.ShapeDtypeStruct((tall, lanes), f32)
    yfirst, ylast = pl.pallas_call(
        columns_kernel,
        grid=(1,),
        out_shape=(plane, plane),
        in_specs=[
            whole(pltpu.SMEM),
            part((layers, rows, lanes), (0, 0, 0)),
            part((layers, rows, lanes), (0, 0, blocks - 1)),
            part((rows, lanes), (0, 0)),
            part((rows, lanes), (0, blocks - 1)),
            part((2, 1, rows, lanes), (0, layers - 1, 0, 0)),
            part((2, 1, rows, lanes), (0, layers - 1, 0, blocks - 1)),
            whole(),
            whole(),
        ],
        out_specs=(whole(), whole()),
        name="columns",
    )(ice_mask, viscosity, viscosity, friction, friction, velocity, velocity, xbefore, xafter)
    ybefore = shift(ylast, "gy", 1)
    yafter = shift(yfirst, "gy", -1)

    coef = pl.pallas_call(
        factors_kernel,
        out_shape=jax.ShapeDtypeStruct((chunks, tiles, FACES, layers, 8, lanes), f32),
        in_specs=[whole(pltpu.SMEM)] + [whole()] * 6,
        out_specs=whole(),
        scratch_shapes=[pltpu.VMEM((layers + 2, tiles, tall, lanes), f32)],
        compiler_params=pltpu.CompilerParams(vmem_limit_bytes=40 * 2**20),
        name="factors",
    )(ice_mask, viscosity, friction, xbefore, xafter, ybefore, yafter)

    pair = jax.ShapeDtypeStruct((2 * tiles, 2, lanes), f32)
    rhs, low, high = pl.pallas_call(
        functools.partial(sources_kernel, slots, layers),
        grid=(1,),
        out_shape=(jax.ShapeDtypeStruct((2, tiles, rows, lanes), f32), pair, pair),
        in_specs=[whole(), part((2, 1, rows, cols), (0, layers - 1, 0, 0)), whole(), whole()],
        out_specs=(whole(), whole(), whole()),
        name="sources",
    )(arrived.reshape(owners * 4 * slots, lanes), velocity, ybefore, yafter)
    before = shift(high, "gx", 1)
    after = shift(low, "gx", -1)

    return pl.pallas_call(
        sweeps_kernel,
        grid=(1,),
        out_shape=(
            jax.ShapeDtypeStruct(velocity.shape, f32),
            jax.ShapeDtypeStruct(friction.shape, f32),
        ),
        in_specs=[whole(pltpu.SMEM), whole(pl.ANY)] + [whole()] * 3 + [part((2, 1, rows, cols), (0, 0, 0, 0))],
        out_specs=(whole(pl.ANY), whole()),
        scratch_shapes=[
            pltpu.VMEM(coef.shape, f32),
            pltpu.VMEM((2, tiles, tall, lanes), f32),
            pltpu.VMEM((2, layers, tiles, tall, lanes), f32),
            pltpu.VMEM((2, layers, tiles, tall, lanes), f32),
            pltpu.VMEM((2, layers, rows, cols), f32),
            pltpu.SemaphoreType.DMA((chunks,)),
            pltpu.SemaphoreType.DMA((chunks - 2,)),
        ],
        compiler_params=pltpu.CompilerParams(vmem_limit_bytes=48 * 2**20),
        name="sweeps",
    )(ice_mask, coef, rhs, before, after, velocity)


def solution(mesh):
    placed = (
        P(None, None, "gx", "gy"),
        P(None, "gx", "gy"),
        P("gx", "gy"),
        P("gx", "gy"),
        P("gx", "gy", None, None, None, None, None),
        P("gx", "gy", None, None, None),
        P("gx", "gy", None, None),
    )
    return jax.shard_map(
        per_device,
        mesh=mesh,
        in_specs=placed,
        out_specs=(P(None, None, "gx", "gy"), P("gx", "gy")),
        check_vma=False,
    )
```

```python
import functools

import jax
import jax.numpy as jnp
from jax import lax
from jax.experimental import pallas as pl
from jax.experimental.pallas import tpu as pltpu
from jax.sharding import PartitionSpec as P

VERTICAL_GAIN = 2.0
RELAX_WEIGHT = 0.8

MARGIN = 8
FACES = 6
MIB = 2**20


def lanes_of(shape):
    return lax.broadcasted_iota(jnp.int32, shape, len(shape) - 1)


def three_parts(value):
    high = value.astype(jnp.bfloat16)
    rest = value - high.astype(jnp.float32)
    middle = rest.astype(jnp.bfloat16)
    low = (rest - middle.astype(jnp.float32)).astype(jnp.bfloat16)
    return jnp.concatenate([high, middle, low], axis=-1)


def sum_parts(value):
    width = value.shape[-1] // 3
    return value[:, :width] + value[:, width : 2 * width] + value[:, 2 * width :]


def pick(onehot, value):
    return sum_parts(jnp.dot(onehot, three_parts(value), preferred_element_type=jnp.float32))


def spread(onehot, value):
    dims = (((0,), (0,)), ((), ()))
    return sum_parts(
        lax.dot_general(onehot, three_parts(value), dims, preferred_element_type=jnp.float32)
    )


def filled(ref, shape):
    return jnp.broadcast_to(ref[...], shape).astype(jnp.float32)


def fetch_all(copies):
    for copy in copies:
        copy.start()


def wait_all(copies):
    for copy in copies:
        copy.wait()


def pack_kernel(
    count_hbm, tiles_hbm, cells_hbm, ice_hbm, visc_hbm, fric_hbm, vel_hbm, out_ref, first_ref, last_ref,
    counts, tiles, cells, ice, visc, fric, vel, sems,
):
    owners_y, owners_x = counts.shape
    slots, lanes = tiles.shape[2], tiles.shape[3]
    layers, rows, cols = visc_hbm.shape
    top = vel_hbm.at[:, vel_hbm.shape[1] - 1]
    ends = (pl.ds(0, lanes), pl.ds(cols - lanes, lanes))
    pairs = [(count_hbm, counts), (cells_hbm, cells), (tiles_hbm, tiles), (ice_hbm, ice)]
    for side, span in enumerate(ends):
        pairs.append((visc_hbm.at[:, :, span], visc.at[side]))
        pairs.append((fric_hbm.at[:, span], fric.at[side]))
        pairs.append((top.at[:, :, span], vel.at[side]))
    copies = [pltpu.make_async_copy(a, b, sems.at[n]) for n, (a, b) in enumerate(pairs)]
    fetch_all(copies)
    wait_all(copies[:3])
    lane = lanes_of((slots, lanes))
    slot = lax.broadcasted_iota(jnp.int32, (slots, lanes), 0)
    zero = jnp.zeros((slots, lanes), jnp.float32)
    for ox in range(owners_x):
        firsts, lasts, owns = [], [], []
        for oy in range(owners_y):
            owner = ox * owners_y + oy
            u = tiles[owner, 0]
            v = tiles[owner, 1]
            count = jnp.broadcast_to(counts[oy : oy + 1, ox : ox + 1], (slots, lanes))
            w = jnp.where(slot < count, tiles[owner, 2], 0.0)
            cell = jnp.broadcast_to(cells[oy, :, ox : ox + 1], (slots, lanes)).astype(jnp.float32)
            out_ref[owner, 0:slots] = u
            out_ref[owner, slots : 2 * slots] = v
            out_ref[owner, 2 * slots : 3 * slots] = w
            first = jnp.where(lane < 4, pltpu.roll(v, 2, 1), jnp.where(lane < 6, pltpu.roll(w, 4, 1), cell))
            firsts.append(jnp.where(lane < 2, u, first))
            last = jnp.where(
                lane >= lanes - 4,
                pltpu.roll(v, lanes - 2, 1),
                jnp.where(lane >= lanes - 6, pltpu.roll(w, lanes - 4, 1), cell),
            )
            lasts.append(jnp.where(lane >= lanes - 2, u, last))
            owns.append(cell)
        for oy in range(owners_y):
            after = firsts[oy + 1] if oy + 1 < owners_y else zero
            before = lasts[oy - 1] if oy > 0 else zero
            meta = jnp.where(lane < 16, after, jnp.where(lane >= lanes - 16, before, owns[oy]))
            out_ref[ox * owners_y + oy, 3 * slots : 4 * slots] = meta

    wait_all(copies[3:])
    lane = lanes_of((rows, lanes))
    icefield = filled(ice, (rows, lanes))
    first = jnp.zeros((rows, lanes), jnp.float32)
    last = jnp.zeros((rows, lanes), jnp.float32)
    for k in range(layers + 4):
        if k < layers:
            mine = (visc[0, k], visc[1, k])
        elif k == layers:
            mine = (fric[0], fric[1])
        elif k == layers + 1:
            mine = (icefield, icefield)
        else:
            mine = (vel[0, k - layers - 2], vel[1, k - layers - 2])
        here = (lane >= 3 * k) & (lane < 3 * k + 3)
        first = jnp.where(here, pltpu.roll(mine[0], 3 * k, 1), first)
        there = (lane >= lanes - 3 - 3 * k) & (lane < lanes - 3 * k)
        last = jnp.where(there, pltpu.roll(mine[1], (lanes - 3 * k) % lanes, 1), last)
    first_ref[...] = first
    last_ref[...] = last


def side_tile(before, after, k):
    lanes = before.shape[-1]
    lane = lanes_of(before.shape)
    left = pltpu.roll(before, (3 * k) % lanes, 1)
    right = pltpu.roll(after, (lanes - 3 * k) % lanes, 1)
    return jnp.where(lane < 3, right, jnp.where(lane >= lanes - 3, left, 0.0))


def ring_pair(load, tile, tiles):
    here = load(tile)
    lanes = here.shape[-1]
    lane = lanes_of(here.shape)
    before = pltpu.roll(jnp.where(lane == lanes - 1, load((tile - 1) % tiles), here), 1, 1)
    after = pltpu.roll(jnp.where(lane == 0, load((tile + 1) % tiles), here), lanes - 1, 1)
    return here, before, after


def factor_columns(layers, tile, tiles, load, store):
    gain = (0.5 * RELAX_WEIGHT) * load(layers + 1, tile, 0)
    up = None
    ratio = None
    for k in range(layers):
        here, south, north = ring_pair(lambda s: load(k, s, 0), tile, tiles)
        west = here + load(k, tile, -1)
        east = here + load(k, tile, 1)
        south = here + south
        north = here + north
        entry = 0.5 * (west + east + south + north)
        if k == 0:
            entry = entry + load(layers, tile, 0)
        if k > 0:
            entry = entry + (up - up * ratio)
        if k < layers - 1:
            above = (0.5 * VERTICAL_GAIN) * (here + load(k + 1, tile, 0))
            entry = entry + above
        inverse = jnp.where(entry > 0.0, 1.0 / entry, 0.0)
        scale = gain * inverse
        store(0, k, west * scale)
        store(1, k, east * scale)
        store(2, k, south * scale)
        store(3, k, north * scale)
        if k > 0:
            store(4, k, up * inverse)
        if k < layers - 1:
            up = above
            ratio = up * inverse
            store(5, k, ratio)
        else:
            store(4, 0, 2.0 * scale)


def first_columns(layers, rhs, coef, store):
    for n in range(2):
        value = rhs(n) * coef(4, 0)
        store(n, layers - 1, value)
        for k in range(layers - 2, -1, -1):
            value = coef(5, k) * value
            store(n, k, value)


def relax_columns(layers, tile, tiles, old, rhs, coef, store):
    forward = [[], []]
    for k in range(layers):
        west, east, south, north = (coef(f, k) for f in range(4))
        for n in range(2):
            here, before, after = ring_pair(lambda s: old(n, k, s, 0), tile, tiles)
            value = west * old(n, k, tile, -1) + east * old(n, k, tile, 1)
            value = value + (south * before + north * after)
            if k > 0:
                value = value + coef(4, k) * forward[n][k - 1]
            if k == layers - 1:
                value = value + rhs(n) * coef(4, 0)
            forward[n].append(value)
    for n in range(2):
        value = forward[n][layers - 1]
        for k in range(layers - 1, -1, -1):
            if k < layers - 1:
                value = forward[n][k] + coef(5, k) * value
            store(n, k, (1.0 - RELAX_WEIGHT) * old(n, k, tile, 0) + value)


def sources_kernel(
    slots, ice_hbm, tiles_ref, visc_hbm, fric_hbm, vel_hbm, before_any, after_any,
    rhs_ref, low_ref, high_ref, xlow_ref, xhigh_ref, ice, visc, fric, vel, before_ref, after_ref, sems,
):
    layers, rows, cols = visc_hbm.shape
    lanes = tiles_ref.shape[1]
    owners = tiles_ref.shape[0] // (4 * slots)
    blocks = cols // lanes
    pairs = [(vel_hbm.at[:, layers - 1], vel), (before_any, before_ref), (after_any, after_ref), (ice_hbm, ice)]
    for side, at in enumerate((0, rows - 8)):
        pairs.append((visc_hbm.at[:, pl.ds(at, 8), :], visc.at[side]))
        pairs.append((fric_hbm.at[pl.ds(at, 8), :], fric.at[side]))
    copies = [pltpu.make_async_copy(a, b, sems.at[n]) for n, (a, b) in enumerate(pairs)]
    fetch_all(copies)

    def channel(c):
        return jnp.concatenate(
            [tiles_ref[pl.ds(c * slots + s, owners, stride=4 * slots), :] for s in range(slots)], axis=0
        )

    seen_u, seen_v, weight, meta = channel(0), channel(1), channel(2), channel(3)
    count = owners * slots
    lane = lanes_of((count, lanes))
    row = lanes_of((count, rows))

    def onehot(column, b):
        cell = jnp.broadcast_to(column.astype(jnp.int32), (count, rows))
        return (cell == row * blocks + b).astype(jnp.bfloat16)

    def put(c, t, plane):
        rhs_ref[c, t] = plane
        xlow_ref[layers + 2 + c, t] = plane[0:4]
        xhigh_ref[layers + 2 + c, t] = plane[rows - 4 : rows]

    own = meta[:, lanes // 2 : lanes // 2 + 1]
    marks = jnp.concatenate([onehot(own, b) for b in range(blocks)], axis=1)
    wait_all(copies[:1])
    surface = jnp.concatenate(
        [
            jnp.concatenate([vel[c, :, b * lanes : (b + 1) * lanes] for b in range(blocks)], axis=0)
            for c in range(2)
        ],
        axis=1,
    )
    weights = jnp.concatenate([weight, weight], axis=1)
    terms = weights * (pick(marks, surface) - jnp.concatenate([seen_u, seen_v], axis=1))
    total = spread(marks, terms)
    for c in range(2):
        for b in range(blocks):
            put(c, b, total[b * rows : (b + 1) * rows, c * lanes : (c + 1) * lanes])

    wait_all(copies[1:3])
    beside = jnp.concatenate(
        [side_tile(before_ref[...], after_ref[...], layers + 2 + c) for c in range(2)], axis=1
    )
    mark_after = onehot(meta[:, 8:9], 0)
    mark_before = onehot(meta[:, lanes - 8 : lanes - 7], blocks - 1)
    weight_after = jnp.where(lane < 2, pltpu.roll(meta, lanes - 4, 1), 0.0)
    weight_before = jnp.where(lane >= lanes - 2, pltpu.roll(meta, 4, 1), 0.0)
    after = jnp.concatenate([meta, pltpu.roll(meta, lanes - 2, 1)], axis=1)
    before = jnp.concatenate([meta, pltpu.roll(meta, 2, 1)], axis=1)
    terms_after = jnp.concatenate([weight_after] * 2, axis=1) * (pick(mark_after, beside) - after)
    terms_before = jnp.concatenate([weight_before] * 2, axis=1) * (pick(mark_before, beside) - before)
    side = spread(mark_after, terms_after) + spread(mark_before, terms_before)
    for c in range(2):
        put(c, blocks, side[:, c * lanes : (c + 1) * lanes])

    wait_all(copies[3:])
    icefield = filled(ice, (8, lanes))
    for k in range(layers + 2):
        for t in range(blocks + 1):
            span = slice(t * lanes, (t + 1) * lanes)
            if t == blocks:
                low = side_tile(before_ref[0:8], after_ref[0:8], k)
                high = side_tile(before_ref[rows - 8 : rows], after_ref[rows - 8 : rows], k)
            elif k < layers:
                low, high = visc[0, k, :, span], visc[1, k, :, span]
            elif k == layers:
                low, high = fric[0, :, span], fric[1, :, span]
            else:
                low, high = icefield, icefield
            low_ref[k, t] = low
            high_ref[k, t] = high
            xlow_ref[k, t] = low[0:4]
            xhigh_ref[k, t] = high[4:8]


def inner_kernel(
    ice_hbm, visc_hbm, fric_hbm, before_any, after_any, rhs_any, adj_hbm, low_ref, high_ref, base_ref,
    ice, field, before, after, rhs, coef, one, two, three, sem_in, sem_out,
):
    steps, tiles, _, layers, _, lanes = coef.shape
    rows = three.shape[3]
    middle = pl.ds(MARGIN, rows)
    pairs = [(ice_hbm, ice), (before_any, before), (after_any, after)]
    for t in range(tiles - 1):
        span = pl.ds(t * lanes, lanes)
        pairs.append((visc_hbm.at[:, :, span], field.at[pl.ds(0, layers), t, middle, :]))
        pairs.append((fric_hbm.at[:, span], field.at[layers, t, middle, :]))
    pairs.append((rhs_any, rhs))
    copies = [pltpu.make_async_copy(a, b, sem_in.at[n]) for n, (a, b) in enumerate(pairs)]
    fetch_all(copies)
    edge = jnp.zeros((MARGIN, lanes), jnp.float32)
    for k in range(layers):
        for t in range(tiles):
            field[k, t, 0:MARGIN] = edge
            field[k, t, MARGIN + rows : 2 * MARGIN + rows] = edge
    wait_all(copies[:3])
    icefield = filled(ice, (rows, lanes))
    for t in range(tiles - 1):
        field[layers + 1, t, middle] = icefield
    for k in range(layers + 2):
        field[k, tiles - 1, middle] = side_tile(before[...], after[...], k)
    wait_all(copies[3:-1])

    def factors(r, carry):
        for t in range(tiles):

            def load(k, s, move):
                return field[k, s, pl.ds(MARGIN + r + move, 8, stride=steps), :]

            def store(f, k, value):
                coef[r, t, f, k] = value

            factor_columns(layers, t, tiles, load, store)
        return carry

    lax.fori_loop(0, steps, factors, 0)
    wait_all(copies[-1:])
    sublane = lax.broadcasted_iota(jnp.int32, (8, lanes), 0)

    def wrap(ref):
        for n in range(2):
            for k in range(layers):
                for t in range(tiles):
                    last = pltpu.roll(ref[n, k, t, steps], 1, 0)
                    ref[n, k, t, 0] = jnp.where(sublane == 0, 0.0, last)
                    first = pltpu.roll(ref[n, k, t, 1], 7, 0)
                    ref[n, k, t, steps + 1] = jnp.where(sublane == 7, 0.0, first)

    def rhs_of(r, t):
        return lambda n: rhs[n, t, pl.ds(r, 8, stride=steps), :]

    def coef_of(r, t):
        return lambda f, k: coef[r, t, f, k]

    def first_sweep(r, carry):
        for t in range(tiles):

            def store(n, k, value):
                one[n, k, t, r + 1] = value

            first_columns(layers, rhs_of(r, t), coef_of(r, t), store)
        return carry

    lax.fori_loop(0, steps, first_sweep, 0, unroll=2)
    wrap(one)

    def second_sweep(r, carry):
        for t in range(tiles):

            def old(n, k, s, move):
                return one[n, k, s, r + 1 + move]

            def store(n, k, value):
                two[n, k, t, r + 1] = value

            relax_columns(layers, t, tiles, old, rhs_of(r, t), coef_of(r, t), store)
        return carry

    lax.fori_loop(0, steps, second_sweep, 0, unroll=2)
    wrap(two)

    def result(t):
        middle = pl.ds(8, rows - 16)
        span = pl.ds(t * lanes, lanes)
        return pltpu.make_async_copy(three.at[:, :, t, middle, :], adj_hbm.at[:, :, middle, span], sem_out.at[t])

    for t in range(tiles - 1):

        def third_sweep(r, carry):
            def old(n, k, s, move):
                return two[n, k, s, r + 1 + move]

            def store(n, k, value):
                three[n, k, t, pl.ds(r, 8, stride=steps), :] = value

            relax_columns(layers, t, tiles, old, rhs_of(r, t), coef_of(r, t), store)
            return carry

        lax.fori_loop(0, steps, third_sweep, 0, unroll=4)
        result(t).start()
        for n in range(2):
            for k in range(layers):
                low_ref[n, k, t] = three[n, k, t, 0:8]
                high_ref[n, k, t] = three[n, k, t, rows - 8 : rows]
        for n in range(2):
            base_ref[n, :, t * lanes : (t + 1) * lanes] = three[n, 0, t]
    for t in range(tiles - 1):
        result(t).wait()


def edges_kernel(
    ice_hbm, own_low, own_high, before_ref, after_ref, rhs_ref, low_ref, high_ref, base_ref, vel_hbm, adj_in,
    adj_hbm, grad_ref, ice, field, coefs, rhs, one, two, patch, vel, sem_in, sem_out,
):
    tiles, _, layers = coefs.shape[1:4]
    rows, cols = grad_ref.shape
    lanes = coefs.shape[5]
    blocks = tiles - 1
    fetches = [
        pltpu.make_async_copy(vel_hbm.at[:, 0], vel, sem_in.at[0]),
        pltpu.make_async_copy(ice_hbm, ice, sem_in.at[1]),
    ]
    fetch_all(fetches)
    for k in range(layers + 4):
        for t in range(tiles):
            if k < layers + 2:
                field[0, k, t, 0:4] = before_ref[k, t]
                field[0, k, t, 4:12] = own_low[k, t]
                field[1, k, t, 4:12] = own_high[k, t]
                field[1, k, t, 12:16] = after_ref[k, t]
            else:
                n = k - layers - 2
                rhs[0, n, t, 0:4] = before_ref[k, t]
                rhs[0, n, t, 4:12] = rhs_ref[n, t, 0:8]
                rhs[1, n, t, 4:12] = rhs_ref[n, t, rows - 8 : rows]
                rhs[1, n, t, 12:16] = after_ref[k, t]
    starts = (2, 6)

    def at(ref, start):
        return lambda *index: ref[(*index, pl.ds(start, 8), slice(None))]

    for t in range(tiles):
        for side in range(2):

            def load(k, s, move):
                return field[side, k, s, pl.ds(starts[side] + move, 8), :]

            def store(f, k, value):
                coefs[side, t, f, k, pl.ds(starts[side], 8), :] = value

            factor_columns(layers, t, tiles, load, store)

    def sides(t, start, side):
        def rhs_of(n):
            return rhs[side, n, t, pl.ds(start, 8), :]

        def coef(f, k):
            return coefs[side, t, f, k, pl.ds(start, 8), :]

        return rhs_of, coef

    for t in range(tiles):
        for side in range(2):
            rhs_of, coef = sides(t, starts[side], side)

            def store(n, k, value):
                one[side, n, k, t, pl.ds(starts[side], 8), :] = value

            first_columns(layers, rhs_of, coef, store)
    for t in range(tiles):
        for side in range(2):
            rhs_of, coef = sides(t, starts[side], side)

            def old(n, k, s, move):
                return one[side, n, k, s, pl.ds(starts[side] + move, 8), :]

            def store(n, k, value):
                two[side, n, k, t, pl.ds(starts[side], 8), :] = value

            relax_columns(layers, t, tiles, old, rhs_of, coef, store)

    def result(side):
        return pltpu.make_async_copy(
            patch.at[side], adj_hbm.at[:, :, pl.ds(side * (rows - 8), 8), :], sem_out.at[side]
        )

    sublane = lax.broadcasted_iota(jnp.int32, (8, lanes), 0)
    wrong = (sublane < 3, sublane >= 5)
    inner = (low_ref, high_ref)
    for side in range(2):
        for t in range(blocks):
            rhs_of, coef = sides(t, 4, side)
            span = slice(t * lanes, (t + 1) * lanes)

            def old(n, k, s, move):
                return two[side, n, k, s, pl.ds(4 + move, 8), :]

            def store(n, k, value):
                patch[side, n, k, :, span] = jnp.where(wrong[side], value, inner[side][n, k, t])

            relax_columns(layers, t, tiles, old, rhs_of, coef, store)
        result(side).start()
    wait_all(fetches)
    icefield = filled(ice, (rows, cols))
    product = base_ref[0] * vel[0] + base_ref[1] * vel[1]
    grad_ref[...] = -icefield * product
    for side in range(2):
        span = slice(side * (rows - 8), side * (rows - 8) + 8)
        product = patch[side, 0, 0] * vel[0, span] + patch[side, 1, 0] * vel[1, span]
        grad_ref[span] = -icefield[0:8] * product
    for side in range(2):
        result(side).wait()


def whole(space=pltpu.VMEM):
    return pl.BlockSpec(memory_space=space)


def per_device(velocity, viscosity, friction, ice_mask, obs_tiles, obs_cell, obs_count):
    layers, rows, cols = viscosity.shape
    owners_x, owners_y, slots, channels, lanes = obs_tiles.shape[2:]
    blocks = cols // lanes
    tiles = blocks + 1
    owners = owners_x * owners_y
    steps = rows // 8
    f32 = jnp.float32

    def shape(*dims):
        return jax.ShapeDtypeStruct(dims, f32)

    def grant(mib):
        return pltpu.CompilerParams(vmem_limit_bytes=int(mib * MIB))

    def shift(value, axis, step):
        size = lax.axis_size(axis)
        pairs = [(i, i + step) for i in range(size) if 0 <= i + step < size]
        return lax.ppermute(value, axis, pairs)

    tiles_in = jnp.transpose(obs_tiles.reshape(owners, slots, channels, lanes), (0, 2, 1, 3))
    cells_in = jnp.transpose(obs_cell[0, 0], (1, 2, 0))
    counts_in = jnp.transpose(obs_count[0, 0], (1, 0))
    def part(dims, *index):
        return pl.BlockSpec(dims, lambda i: index)

    i32 = jnp.int32
    plane = shape(rows, lanes)
    hbm = whole(pltpu.HBM)
    anywhere = whole(pl.ANY)
    packed, yfirst, ylast = pl.pallas_call(
        pack_kernel,
        out_shape=(shape(owners, 4 * slots, lanes), plane, plane),
        in_specs=[hbm] * 7,
        out_specs=(whole(),) * 3,
        scratch_shapes=[
            pltpu.VMEM(counts_in.shape, i32),
            pltpu.VMEM(tiles_in.shape, f32),
            pltpu.VMEM(cells_in.shape, i32),
            pltpu.VMEM((1, 1), i32),
            pltpu.VMEM((2, layers, rows, lanes), f32),
            pltpu.VMEM((2, rows, lanes), f32),
            pltpu.VMEM((2, 2, rows, lanes), f32),
            pltpu.SemaphoreType.DMA((10,)),
        ],
        compiler_params=grant(62.5),
        cost_estimate=pl.CostEstimate(flops=4 * 10**9, transcendentals=0, bytes_accessed=0),
        name="pack",
    )(counts_in, tiles_in, cells_in, ice_mask, viscosity, friction, velocity)
    arrived = lax.all_to_all(packed, ("gx", "gy"), split_axis=0, concat_axis=0, tiled=True)
    ybefore = shift(ylast, "gy", 1)
    yafter = shift(yfirst, "gy", -1)

    own = shape(layers + 2, tiles, 8, lanes)
    edge = shape(layers + 4, tiles, 4, lanes)
    rhs, own_low, own_high, xlow, xhigh = pl.pallas_call(
        functools.partial(sources_kernel, slots),
        out_shape=(shape(2, tiles, rows, lanes), own, own, edge, edge),
        in_specs=[hbm, whole(), hbm, hbm, hbm, anywhere, anywhere],
        out_specs=(whole(),) * 5,
        scratch_shapes=[
            pltpu.VMEM((1, 1), i32),
            pltpu.VMEM((2, layers, 8, cols), f32),
            pltpu.VMEM((2, 8, cols), f32),
            pltpu.VMEM((2, rows, cols), f32),
            pltpu.VMEM((rows, lanes), f32),
            pltpu.VMEM((rows, lanes), f32),
            pltpu.SemaphoreType.DMA((8,)),
        ],
        compiler_params=grant(12 + (owners * slots) // 64),
        cost_estimate=pl.CostEstimate(flops=4 * 10**9, transcendentals=0, bytes_accessed=0),
        name="sources",
    )(ice_mask, arrived.reshape(owners * 4 * slots, lanes), viscosity, friction, velocity, ybefore, yafter)
    xbefore = shift(xhigh, "gx", 1)
    xafter = shift(xlow, "gx", -1)

    ends = shape(2, layers, blocks, 8, lanes)
    wide = pltpu.VMEM((2, layers, tiles, steps + 2, 8, lanes), f32)
    adjoint, low, high, base = pl.pallas_call(
        inner_kernel,
        out_shape=(shape(*velocity.shape), ends, ends, shape(2, rows, cols)),
        in_specs=[hbm, hbm, hbm, anywhere, anywhere, anywhere],
        out_specs=(hbm, whole(), whole(), whole()),
        scratch_shapes=[
            pltpu.VMEM((1, 1), i32),
            pltpu.VMEM((layers + 2, tiles, rows + 2 * MARGIN, lanes), f32),
            pltpu.VMEM((rows, lanes), f32),
            pltpu.VMEM((rows, lanes), f32),
            pltpu.VMEM((2, tiles, rows, lanes), f32),
            pltpu.VMEM((steps, tiles, FACES, layers, 8, lanes), f32),
            wide,
            wide,
            pltpu.VMEM((2, layers, blocks, rows, lanes), f32),
            pltpu.SemaphoreType.DMA((2 * blocks + 4,)),
            pltpu.SemaphoreType.DMA((blocks,)),
        ],
        compiler_params=grant(30),
        cost_estimate=pl.CostEstimate(flops=4 * 10**9, transcendentals=0, bytes_accessed=0),
        name="inner",
    )(ice_mask, viscosity, friction, ybefore, yafter, rhs)

    return pl.pallas_call(
        edges_kernel,
        out_shape=(shape(*velocity.shape), shape(rows, cols)),
        in_specs=[hbm] + [whole()] * 8 + [hbm, hbm],
        out_specs=(hbm, whole()),
        scratch_shapes=[
            pltpu.VMEM((1, 1), i32),
            pltpu.VMEM((2, layers + 2, tiles, 16, lanes), f32),
            pltpu.VMEM((2, tiles, FACES, layers, 16, lanes), f32),
            pltpu.VMEM((2, 2, tiles, 16, lanes), f32),
            pltpu.VMEM((2, 2, layers, tiles, 16, lanes), f32),
            pltpu.VMEM((2, 2, layers, tiles, 16, lanes), f32),
            pltpu.VMEM((2, 2, layers, 8, cols), f32),
            pltpu.VMEM((2, rows, cols), f32),
            pltpu.SemaphoreType.DMA((2,)),
            pltpu.SemaphoreType.DMA((2,)),
        ],
        input_output_aliases={10: 0},
        compiler_params=grant(14),
        cost_estimate=pl.CostEstimate(flops=4 * 10**9, transcendentals=0, bytes_accessed=0),
        name="edges",
    )(ice_mask, own_low, own_high, xbefore, xafter, rhs, low, high, base, velocity, adjoint)


def solution(mesh):
    placed = (
        P(None, None, "gx", "gy"),
        P(None, "gx", "gy"),
        P("gx", "gy"),
        P("gx", "gy"),
        P("gx", "gy", None, None, None, None, None),
        P("gx", "gy", None, None, None),
        P("gx", "gy", None, None),
    )
    return jax.shard_map(
        per_device,
        mesh=mesh,
        in_specs=placed,
        out_specs=(P(None, None, "gx", "gy"), P("gx", "gy")),
        check_vma=False,
    )
```

```python
import functools

import jax
import jax.numpy as jnp
from jax import lax
from jax.experimental import pallas as pl
from jax.experimental.pallas import tpu as pltpu
from jax.sharding import PartitionSpec as P

VERTICAL_GAIN = 2.0
RELAX_WEIGHT = 0.8

MARGIN = 8
FACES = 6
MIB = 2**20


def lanes_of(shape):
    return lax.broadcasted_iota(jnp.int32, shape, len(shape) - 1)


def three_parts(value):
    high = value.astype(jnp.bfloat16)
    rest = value - high.astype(jnp.float32)
    middle = rest.astype(jnp.bfloat16)
    low = (rest - middle.astype(jnp.float32)).astype(jnp.bfloat16)
    return jnp.concatenate([high, middle, low], axis=-1)


def sum_parts(value):
    width = value.shape[-1] // 3
    return value[:, :width] + value[:, width : 2 * width] + value[:, 2 * width :]


def pick(onehot, value):
    return sum_parts(jnp.dot(onehot, three_parts(value), preferred_element_type=jnp.float32))


def spread(onehot, value):
    dims = (((0,), (0,)), ((), ()))
    return sum_parts(
        lax.dot_general(onehot, three_parts(value), dims, preferred_element_type=jnp.float32)
    )


def filled(ref, shape):
    return jnp.broadcast_to(ref[...], shape).astype(jnp.float32)


def is_even(axis):
    return lax.rem(lax.axis_index(axis), 2) == 0


def received(axis, one, two):
    even = is_even(axis)
    return jnp.where(even, two, one), jnp.where(even, one, two)


def fetch_all(copies):
    for copy in copies:
        copy.start()


def wait_all(copies):
    for copy in copies:
        copy.wait()


def pack_kernel(count_hbm, tiles_hbm, cells_hbm, out_ref, counts, tiles, cells, sems):
    owners_y, owners_x = counts.shape
    slots, lanes = tiles.shape[2], tiles.shape[3]
    pairs = [(count_hbm, counts), (cells_hbm, cells), (tiles_hbm, tiles)]
    copies = [pltpu.make_async_copy(a, b, sems.at[n]) for n, (a, b) in enumerate(pairs)]
    fetch_all(copies)
    wait_all(copies)
    lane = lanes_of((slots, lanes))
    slot = lax.broadcasted_iota(jnp.int32, (slots, lanes), 0)
    zero = jnp.zeros((slots, lanes), jnp.float32)
    for ox in range(owners_x):
        firsts, lasts, owns = [], [], []
        for oy in range(owners_y):
            owner = ox * owners_y + oy
            u = tiles[owner, 0]
            v = tiles[owner, 1]
            count = jnp.broadcast_to(counts[oy : oy + 1, ox : ox + 1], (slots, lanes))
            w = jnp.where(slot < count, tiles[owner, 2], 0.0)
            cell = jnp.broadcast_to(cells[oy, :, ox : ox + 1], (slots, lanes)).astype(jnp.float32)
            out_ref[owner, 0:slots] = u
            out_ref[owner, slots : 2 * slots] = v
            out_ref[owner, 2 * slots : 3 * slots] = w
            first = jnp.where(lane < 4, pltpu.roll(v, 2, 1), jnp.where(lane < 6, pltpu.roll(w, 4, 1), cell))
            firsts.append(jnp.where(lane < 2, u, first))
            last = jnp.where(
                lane >= lanes - 4,
                pltpu.roll(v, lanes - 2, 1),
                jnp.where(lane >= lanes - 6, pltpu.roll(w, lanes - 4, 1), cell),
            )
            lasts.append(jnp.where(lane >= lanes - 2, u, last))
            owns.append(cell)
        for oy in range(owners_y):
            after = firsts[oy + 1] if oy + 1 < owners_y else zero
            before = lasts[oy - 1] if oy > 0 else zero
            meta = jnp.where(lane < 16, after, jnp.where(lane >= lanes - 16, before, owns[oy]))
            out_ref[ox * owners_y + oy, 3 * slots : 4 * slots] = meta


def columns_kernel(ice_hbm, visc_hbm, fric_hbm, vel_hbm, one_ref, two_ref, ice, visc, fric, vel, sems):
    layers, rows, cols = visc_hbm.shape
    lanes = one_ref.shape[1]
    top = vel_hbm.at[:, vel_hbm.shape[1] - 1]
    pairs = [(ice_hbm, ice)]
    for side, span in enumerate((pl.ds(0, lanes), pl.ds(cols - lanes, lanes))):
        pairs.append((visc_hbm.at[:, :, span], visc.at[side]))
        pairs.append((fric_hbm.at[:, span], fric.at[side]))
        pairs.append((top.at[:, :, span], vel.at[side]))
    copies = [pltpu.make_async_copy(a, b, sems.at[n]) for n, (a, b) in enumerate(pairs)]
    fetch_all(copies)
    wait_all(copies)
    lane = lanes_of((rows, lanes))
    icefield = filled(ice, (rows, lanes))
    first = jnp.zeros((rows, lanes), jnp.float32)
    last = jnp.zeros((rows, lanes), jnp.float32)
    for k in range(layers + 4):
        if k < layers:
            mine = (visc[0, k], visc[1, k])
        elif k == layers:
            mine = (fric[0], fric[1])
        elif k == layers + 1:
            mine = (icefield, icefield)
        else:
            mine = (vel[0, k - layers - 2], vel[1, k - layers - 2])
        here = (lane >= 3 * k) & (lane < 3 * k + 3)
        first = jnp.where(here, pltpu.roll(mine[0], 3 * k, 1), first)
        there = (lane >= lanes - 3 - 3 * k) & (lane < lanes - 3 * k)
        last = jnp.where(there, pltpu.roll(mine[1], (lanes - 3 * k) % lanes, 1), last)
    even = is_even("gy")
    one_ref[...] = jnp.where(even, last, first)
    two_ref[...] = jnp.where(even, first, last)


def side_tile(before, after, k):
    lanes = before.shape[-1]
    lane = lanes_of(before.shape)
    left = pltpu.roll(before, (3 * k) % lanes, 1)
    right = pltpu.roll(after, (lanes - 3 * k) % lanes, 1)
    return jnp.where(lane < 3, right, jnp.where(lane >= lanes - 3, left, 0.0))


def ring_pair(load, tile, tiles):
    here = load(tile)
    lanes = here.shape[-1]
    lane = lanes_of(here.shape)
    before = pltpu.roll(jnp.where(lane == lanes - 1, load((tile - 1) % tiles), here), 1, 1)
    after = pltpu.roll(jnp.where(lane == 0, load((tile + 1) % tiles), here), lanes - 1, 1)
    return here, before, after


def factor_columns(layers, tile, tiles, load, store):
    gain = (0.5 * RELAX_WEIGHT) * load(layers + 1, tile, 0)
    up = None
    ratio = None
    for k in range(layers):
        here, south, north = ring_pair(lambda s: load(k, s, 0), tile, tiles)
        west = here + load(k, tile, -1)
        east = here + load(k, tile, 1)
        south = here + south
        north = here + north
        entry = 0.5 * (west + east + south + north)
        if k == 0:
            entry = entry + load(layers, tile, 0)
        if k > 0:
            entry = entry + (up - up * ratio)
        if k < layers - 1:
            above = (0.5 * VERTICAL_GAIN) * (here + load(k + 1, tile, 0))
            entry = entry + above
        inverse = jnp.where(entry > 0.0, 1.0 / entry, 0.0)
        scale = gain * inverse
        store(0, k, west * scale)
        store(1, k, east * scale)
        store(2, k, south * scale)
        store(3, k, north * scale)
        if k > 0:
            store(4, k, up * inverse)
        if k < layers - 1:
            up = above
            ratio = up * inverse
            store(5, k, ratio)
        else:
            store(4, 0, 2.0 * scale)


def first_columns(layers, rhs, coef, store):
    for n in range(2):
        value = rhs(n) * coef(4, 0)
        store(n, layers - 1, value)
        for k in range(layers - 2, -1, -1):
            value = coef(5, k) * value
            store(n, k, value)


def relax_columns(layers, tile, tiles, old, rhs, coef, store):
    forward = [[], []]
    for k in range(layers):
        west, east, south, north = (coef(f, k) for f in range(4))
        for n in range(2):
            here, before, after = ring_pair(lambda s: old(n, k, s, 0), tile, tiles)
            value = west * old(n, k, tile, -1) + east * old(n, k, tile, 1)
            value = value + (south * before + north * after)
            if k > 0:
                value = value + coef(4, k) * forward[n][k - 1]
            if k == layers - 1:
                value = value + rhs(n) * coef(4, 0)
            forward[n].append(value)
    for n in range(2):
        value = forward[n][layers - 1]
        for k in range(layers - 1, -1, -1):
            if k < layers - 1:
                value = forward[n][k] + coef(5, k) * value
            store(n, k, (1.0 - RELAX_WEIGHT) * old(n, k, tile, 0) + value)


def sources_kernel(
    slots, ice_hbm, tiles_ref, visc_hbm, fric_hbm, vel_hbm, one_any, two_any,
    rhs_ref, low_ref, high_ref, xone_ref, xtwo_ref, ice, visc, fric, vel, one, two, sems,
):
    layers, rows, cols = visc_hbm.shape
    lanes = tiles_ref.shape[1]
    owners = tiles_ref.shape[0] // (4 * slots)
    blocks = cols // lanes
    pairs = [(vel_hbm.at[:, layers - 1], vel), (one_any, one), (two_any, two), (ice_hbm, ice)]
    for side, at in enumerate((0, rows - 8)):
        pairs.append((visc_hbm.at[:, pl.ds(at, 8), :], visc.at[side]))
        pairs.append((fric_hbm.at[pl.ds(at, 8), :], fric.at[side]))
    copies = [pltpu.make_async_copy(a, b, sems.at[n]) for n, (a, b) in enumerate(pairs)]
    fetch_all(copies)

    def channel(c):
        return jnp.concatenate(
            [tiles_ref[pl.ds(c * slots + s, owners, stride=4 * slots), :] for s in range(slots)], axis=0
        )

    seen_u, seen_v, weight, meta = channel(0), channel(1), channel(2), channel(3)
    count = owners * slots
    lane = lanes_of((count, lanes))
    row = lanes_of((count, rows))

    def onehot(column, b):
        cell = jnp.broadcast_to(column.astype(jnp.int32), (count, rows))
        return (cell == row * blocks + b).astype(jnp.bfloat16)

    even = is_even("gx")

    def send(k, t, low, high):
        xone_ref[k, t] = jnp.where(even, high, low)
        xtwo_ref[k, t] = jnp.where(even, low, high)

    def put(c, t, plane):
        rhs_ref[c, t] = plane
        send(layers + 2 + c, t, plane[0:4], plane[rows - 4 : rows])

    own = meta[:, lanes // 2 : lanes // 2 + 1]
    marks = jnp.concatenate([onehot(own, b) for b in range(blocks)], axis=1)
    wait_all(copies[:1])
    surface = jnp.concatenate(
        [
            jnp.concatenate([vel[c, :, b * lanes : (b + 1) * lanes] for b in range(blocks)], axis=0)
            for c in range(2)
        ],
        axis=1,
    )
    weights = jnp.concatenate([weight, weight], axis=1)
    terms = weights * (pick(marks, surface) - jnp.concatenate([seen_u, seen_v], axis=1))
    total = spread(marks, terms)
    for c in range(2):
        for b in range(blocks):
            put(c, b, total[b * rows : (b + 1) * rows, c * lanes : (c + 1) * lanes])

    wait_all(copies[1:3])
    before_ref, after_ref = received("gy", one[...], two[...])
    beside = jnp.concatenate(
        [side_tile(before_ref, after_ref, layers + 2 + c) for c in range(2)], axis=1
    )
    mark_after = onehot(meta[:, 8:9], 0)
    mark_before = onehot(meta[:, lanes - 8 : lanes - 7], blocks - 1)
    weight_after = jnp.where(lane < 2, pltpu.roll(meta, lanes - 4, 1), 0.0)
    weight_before = jnp.where(lane >= lanes - 2, pltpu.roll(meta, 4, 1), 0.0)
    after = jnp.concatenate([meta, pltpu.roll(meta, lanes - 2, 1)], axis=1)
    before = jnp.concatenate([meta, pltpu.roll(meta, 2, 1)], axis=1)
    terms_after = jnp.concatenate([weight_after] * 2, axis=1) * (pick(mark_after, beside) - after)
    terms_before = jnp.concatenate([weight_before] * 2, axis=1) * (pick(mark_before, beside) - before)
    side = spread(mark_after, terms_after) + spread(mark_before, terms_before)
    for c in range(2):
        put(c, blocks, side[:, c * lanes : (c + 1) * lanes])

    wait_all(copies[3:])
    icefield = filled(ice, (8, lanes))
    for k in range(layers + 2):
        for t in range(blocks + 1):
            span = slice(t * lanes, (t + 1) * lanes)
            if t == blocks:
                low = side_tile(before_ref[0:8], after_ref[0:8], k)
                high = side_tile(before_ref[rows - 8 : rows], after_ref[rows - 8 : rows], k)
            elif k < layers:
                low, high = visc[0, k, :, span], visc[1, k, :, span]
            elif k == layers:
                low, high = fric[0, :, span], fric[1, :, span]
            else:
                low, high = icefield, icefield
            low_ref[k, t] = low
            high_ref[k, t] = high
            send(k, t, low[0:4], high[4:8])


def inner_kernel(
    ice_hbm, visc_hbm, fric_hbm, one_any, two_any, rhs_any, adj_hbm, low_ref, high_ref, base_ref,
    ice, field, swap_one, swap_two, rhs, coef, one, two, three, sem_in, sem_out,
):
    steps, tiles, _, layers, _, lanes = coef.shape
    rows = three.shape[3]
    middle = pl.ds(MARGIN, rows)
    pairs = [(ice_hbm, ice), (one_any, swap_one), (two_any, swap_two)]
    for t in range(tiles - 1):
        span = pl.ds(t * lanes, lanes)
        pairs.append((visc_hbm.at[:, :, span], field.at[pl.ds(0, layers), t, middle, :]))
        pairs.append((fric_hbm.at[:, span], field.at[layers, t, middle, :]))
    pairs.append((rhs_any, rhs))
    copies = [pltpu.make_async_copy(a, b, sem_in.at[n]) for n, (a, b) in enumerate(pairs)]
    fetch_all(copies)
    edge = jnp.zeros((MARGIN, lanes), jnp.float32)
    for k in range(layers):
        for t in range(tiles):
            field[k, t, 0:MARGIN] = edge
            field[k, t, MARGIN + rows : 2 * MARGIN + rows] = edge
    wait_all(copies[:3])
    icefield = filled(ice, (rows, lanes))
    for t in range(tiles - 1):
        field[layers + 1, t, middle] = icefield
    before, after = received("gy", swap_one[...], swap_two[...])
    for k in range(layers + 2):
        field[k, tiles - 1, middle] = side_tile(before, after, k)
    wait_all(copies[3:-1])

    def factors(r, carry):
        for t in range(tiles):

            def load(k, s, move):
                return field[k, s, pl.ds(MARGIN + r + move, 8, stride=steps), :]

            def store(f, k, value):
                coef[r, t, f, k] = value

            factor_columns(layers, t, tiles, load, store)
        return carry

    lax.fori_loop(0, steps, factors, 0, unroll=3)
    wait_all(copies[-1:])
    sublane = lax.broadcasted_iota(jnp.int32, (8, lanes), 0)

    def wrap(ref):
        for n in range(2):
            for k in range(layers):
                for t in range(tiles):
                    last = pltpu.roll(ref[n, k, t, steps], 1, 0)
                    ref[n, k, t, 0] = jnp.where(sublane == 0, 0.0, last)
                    first = pltpu.roll(ref[n, k, t, 1], 7, 0)
                    ref[n, k, t, steps + 1] = jnp.where(sublane == 7, 0.0, first)

    def rhs_of(r, t):
        return lambda n: rhs[n, t, pl.ds(r, 8, stride=steps), :]

    def coef_of(r, t):
        return lambda f, k: coef[r, t, f, k]

    def first_sweep(r, carry):
        for t in range(tiles):

            def store(n, k, value):
                one[n, k, t, r + 1] = value

            first_columns(layers, rhs_of(r, t), coef_of(r, t), store)
        return carry

    lax.fori_loop(0, steps, first_sweep, 0, unroll=2)
    wrap(one)

    def second_sweep(r, carry):
        for t in range(tiles):

            def old(n, k, s, move):
                return one[n, k, s, r + 1 + move]

            def store(n, k, value):
                two[n, k, t, r + 1] = value

            relax_columns(layers, t, tiles, old, rhs_of(r, t), coef_of(r, t), store)
        return carry

    lax.fori_loop(0, steps, second_sweep, 0, unroll=4)
    wrap(two)

    def result(t):
        middle = pl.ds(8, rows - 16)
        span = pl.ds(t * lanes, lanes)
        return pltpu.make_async_copy(three.at[:, :, t, middle, :], adj_hbm.at[:, :, middle, span], sem_out.at[t])

    for t in range(tiles - 1):

        def third_sweep(r, carry):
            def old(n, k, s, move):
                return two[n, k, s, r + 1 + move]

            def store(n, k, value):
                three[n, k, t, pl.ds(r, 8, stride=steps), :] = value

            relax_columns(layers, t, tiles, old, rhs_of(r, t), coef_of(r, t), store)
            return carry

        lax.fori_loop(0, steps, third_sweep, 0, unroll=12)
        result(t).start()
        for n in range(2):
            for k in range(layers):
                low_ref[n, k, t] = three[n, k, t, 0:8]
                high_ref[n, k, t] = three[n, k, t, rows - 8 : rows]
        for n in range(2):
            base_ref[n, :, t * lanes : (t + 1) * lanes] = three[n, 0, t]
    for t in range(tiles - 1):
        result(t).wait()


def edges_kernel(
    ice_hbm, own_low, own_high, one_ref, two_ref, rhs_ref, low_ref, high_ref, base_ref, vel_hbm, adj_in,
    adj_hbm, grad_ref, ice, field, coefs, rhs, one, two, patch, vel, sem_in, sem_out,
):
    tiles, _, layers = coefs.shape[1:4]
    rows, cols = grad_ref.shape
    lanes = coefs.shape[5]
    blocks = tiles - 1
    fetches = [
        pltpu.make_async_copy(vel_hbm.at[:, 0], vel, sem_in.at[0]),
        pltpu.make_async_copy(ice_hbm, ice, sem_in.at[1]),
    ]
    fetch_all(fetches)
    for k in range(layers + 4):
        for t in range(tiles):
            before, after = received("gx", one_ref[k, t], two_ref[k, t])
            if k < layers + 2:
                field[0, k, t, 0:4] = before
                field[0, k, t, 4:12] = own_low[k, t]
                field[1, k, t, 4:12] = own_high[k, t]
                field[1, k, t, 12:16] = after
            else:
                n = k - layers - 2
                rhs[0, n, t, 0:4] = before
                rhs[0, n, t, 4:12] = rhs_ref[n, t, 0:8]
                rhs[1, n, t, 4:12] = rhs_ref[n, t, rows - 8 : rows]
                rhs[1, n, t, 12:16] = after
    starts = (2, 6)

    def at(ref, start):
        return lambda *index: ref[(*index, pl.ds(start, 8), slice(None))]

    for t in range(tiles):
        for side in range(2):

            def load(k, s, move):
                return field[side, k, s, pl.ds(starts[side] + move, 8), :]

            def store(f, k, value):
                coefs[side, t, f, k, pl.ds(starts[side], 8), :] = value

            factor_columns(layers, t, tiles, load, store)

    def sides(t, start, side):
        def rhs_of(n):
            return rhs[side, n, t, pl.ds(start, 8), :]

        def coef(f, k):
            return coefs[side, t, f, k, pl.ds(start, 8), :]

        return rhs_of, coef

    for t in range(tiles):
        for side in range(2):
            rhs_of, coef = sides(t, starts[side], side)

            def store(n, k, value):
                one[side, n, k, t, pl.ds(starts[side], 8), :] = value

            first_columns(layers, rhs_of, coef, store)
    for t in range(tiles):
        for side in range(2):
            rhs_of, coef = sides(t, starts[side], side)

            def old(n, k, s, move):
                return one[side, n, k, s, pl.ds(starts[side] + move, 8), :]

            def store(n, k, value):
                two[side, n, k, t, pl.ds(starts[side], 8), :] = value

            relax_columns(layers, t, tiles, old, rhs_of, coef, store)

    def result(side):
        return pltpu.make_async_copy(
            patch.at[side], adj_hbm.at[:, :, pl.ds(side * (rows - 8), 8), :], sem_out.at[side]
        )

    sublane = lax.broadcasted_iota(jnp.int32, (8, lanes), 0)
    wrong = (sublane < 3, sublane >= 5)
    inner = (low_ref, high_ref)
    for side in range(2):
        for t in range(blocks):
            rhs_of, coef = sides(t, 4, side)
            span = slice(t * lanes, (t + 1) * lanes)

            def old(n, k, s, move):
                return two[side, n, k, s, pl.ds(4 + move, 8), :]

            def store(n, k, value):
                patch[side, n, k, :, span] = jnp.where(wrong[side], value, inner[side][n, k, t])

            relax_columns(layers, t, tiles, old, rhs_of, coef, store)
        result(side).start()
    wait_all(fetches)
    icefield = filled(ice, (rows, cols))
    product = base_ref[0] * vel[0] + base_ref[1] * vel[1]
    grad_ref[...] = -icefield * product
    for side in range(2):
        span = slice(side * (rows - 8), side * (rows - 8) + 8)
        product = patch[side, 0, 0] * vel[0, span] + patch[side, 1, 0] * vel[1, span]
        grad_ref[span] = -icefield[0:8] * product
    for side in range(2):
        result(side).wait()


def whole(space=pltpu.VMEM):
    return pl.BlockSpec(memory_space=space)


def per_device(velocity, viscosity, friction, ice_mask, obs_tiles, obs_cell, obs_count):
    layers, rows, cols = viscosity.shape
    owners_x, owners_y, slots, channels, lanes = obs_tiles.shape[2:]
    blocks = cols // lanes
    tiles = blocks + 1
    owners = owners_x * owners_y
    steps = rows // 8
    f32 = jnp.float32

    def shape(*dims):
        return jax.ShapeDtypeStruct(dims, f32)

    def grant(mib):
        return pltpu.CompilerParams(vmem_limit_bytes=int(mib * MIB))

    def swap(value, axis, first):
        pairs = []
        for i in range(first, lax.axis_size(axis) - 1, 2):
            pairs += [(i, i + 1), (i + 1, i)]
        return lax.ppermute(value, axis, pairs)

    tiles_in = jnp.transpose(obs_tiles.reshape(owners, slots, channels, lanes), (0, 2, 1, 3))
    cells_in = jnp.transpose(obs_cell[0, 0], (1, 2, 0))
    counts_in = jnp.transpose(obs_count[0, 0], (1, 0))
    def part(dims, *index):
        return pl.BlockSpec(dims, lambda i: index)

    i32 = jnp.int32
    plane = shape(rows, lanes)
    hbm = whole(pltpu.HBM)
    anywhere = whole(pl.ANY)
    packed = pl.pallas_call(
        pack_kernel,
        out_shape=shape(owners, 4 * slots, lanes),
        in_specs=[hbm] * 3,
        out_specs=whole(),
        scratch_shapes=[
            pltpu.VMEM(counts_in.shape, i32),
            pltpu.VMEM(tiles_in.shape, f32),
            pltpu.VMEM(cells_in.shape, i32),
            pltpu.SemaphoreType.DMA((3,)),
        ],
        compiler_params=grant(62.5),
        cost_estimate=pl.CostEstimate(flops=4 * 10**9, transcendentals=0, bytes_accessed=0),
        name="pack",
    )(counts_in, tiles_in, cells_in)
    arrived = lax.all_to_all(packed, ("gx", "gy"), split_axis=0, concat_axis=0, tiled=True)
    ysend_one, ysend_two = pl.pallas_call(
        columns_kernel,
        out_shape=(plane, plane),
        in_specs=[hbm] * 4,
        out_specs=(whole(), whole()),
        scratch_shapes=[
            pltpu.VMEM((1, 1), i32),
            pltpu.VMEM((2, layers, rows, lanes), f32),
            pltpu.VMEM((2, rows, lanes), f32),
            pltpu.VMEM((2, 2, rows, lanes), f32),
            pltpu.SemaphoreType.DMA((7,)),
        ],
        compiler_params=grant(62.5),
        cost_estimate=pl.CostEstimate(flops=4 * 10**9, transcendentals=0, bytes_accessed=0),
        name="columns",
    )(ice_mask, viscosity, friction, velocity)
    yone = swap(ysend_one, "gy", 0)
    ytwo = swap(ysend_two, "gy", 1)

    own = shape(layers + 2, tiles, 8, lanes)
    edge = shape(layers + 4, tiles, 4, lanes)
    rhs, own_low, own_high, xsend_one, xsend_two = pl.pallas_call(
        functools.partial(sources_kernel, slots),
        out_shape=(shape(2, tiles, rows, lanes), own, own, edge, edge),
        in_specs=[hbm, whole(), hbm, hbm, hbm, anywhere, anywhere],
        out_specs=(whole(),) * 5,
        scratch_shapes=[
            pltpu.VMEM((1, 1), i32),
            pltpu.VMEM((2, layers, 8, cols), f32),
            pltpu.VMEM((2, 8, cols), f32),
            pltpu.VMEM((2, rows, cols), f32),
            pltpu.VMEM((rows, lanes), f32),
            pltpu.VMEM((rows, lanes), f32),
            pltpu.SemaphoreType.DMA((8,)),
        ],
        compiler_params=grant(52),
        cost_estimate=pl.CostEstimate(flops=4 * 10**9, transcendentals=0, bytes_accessed=0),
        name="sources",
    )(ice_mask, arrived.reshape(owners * 4 * slots, lanes), viscosity, friction, velocity, yone, ytwo)
    xone = swap(xsend_one, "gx", 0)
    xtwo = swap(xsend_two, "gx", 1)

    ends = shape(2, layers, blocks, 8, lanes)
    wide = pltpu.VMEM((2, layers, tiles, steps + 2, 8, lanes), f32)
    adjoint, low, high, base = pl.pallas_call(
        inner_kernel,
        out_shape=(shape(*velocity.shape), ends, ends, shape(2, rows, cols)),
        in_specs=[hbm, hbm, hbm, anywhere, anywhere, anywhere],
        out_specs=(hbm, whole(), whole(), whole()),
        scratch_shapes=[
            pltpu.VMEM((1, 1), i32),
            pltpu.VMEM((layers + 2, tiles, rows + 2 * MARGIN, lanes), f32),
            pltpu.VMEM((rows, lanes), f32),
            pltpu.VMEM((rows, lanes), f32),
            pltpu.VMEM((2, tiles, rows, lanes), f32),
            pltpu.VMEM((steps, tiles, FACES, layers, 8, lanes), f32),
            wide,
            wide,
            pltpu.VMEM((2, layers, blocks, rows, lanes), f32),
            pltpu.SemaphoreType.DMA((2 * blocks + 4,)),
            pltpu.SemaphoreType.DMA((blocks,)),
        ],
        compiler_params=grant(30),
        cost_estimate=pl.CostEstimate(flops=4 * 10**9, transcendentals=0, bytes_accessed=0),
        name="inner",
    )(ice_mask, viscosity, friction, yone, ytwo, rhs)

    return pl.pallas_call(
        edges_kernel,
        out_shape=(shape(*velocity.shape), shape(rows, cols)),
        in_specs=[hbm] + [whole()] * 8 + [hbm, hbm],
        out_specs=(hbm, whole()),
        scratch_shapes=[
            pltpu.VMEM((1, 1), i32),
            pltpu.VMEM((2, layers + 2, tiles, 16, lanes), f32),
            pltpu.VMEM((2, tiles, FACES, layers, 16, lanes), f32),
            pltpu.VMEM((2, 2, tiles, 16, lanes), f32),
            pltpu.VMEM((2, 2, layers, tiles, 16, lanes), f32),
            pltpu.VMEM((2, 2, layers, tiles, 16, lanes), f32),
            pltpu.VMEM((2, 2, layers, 8, cols), f32),
            pltpu.VMEM((2, rows, cols), f32),
            pltpu.SemaphoreType.DMA((2,)),
            pltpu.SemaphoreType.DMA((2,)),
        ],
        input_output_aliases={10: 0},
        compiler_params=grant(14),
        cost_estimate=pl.CostEstimate(flops=4 * 10**9, transcendentals=0, bytes_accessed=0),
        name="edges",
    )(ice_mask, own_low, own_high, xone, xtwo, rhs, low, high, base, velocity, adjoint)


def solution(mesh):
    placed = (
        P(None, None, "gx", "gy"),
        P(None, "gx", "gy"),
        P("gx", "gy"),
        P("gx", "gy"),
        P("gx", "gy", None, None, None, None, None),
        P("gx", "gy", None, None, None),
        P("gx", "gy", None, None),
    )
    return jax.shard_map(
        per_device,
        mesh=mesh,
        in_specs=placed,
        out_specs=(P(None, None, "gx", "gy"), P("gx", "gy")),
        check_vma=False,
    )
```

```python
import functools

import jax
import jax.numpy as jnp
from jax import lax
from jax.experimental import pallas as pl
from jax.experimental.pallas import tpu as pltpu
from jax.sharding import PartitionSpec as P

VERTICAL_GAIN = 2.0
RELAX_WEIGHT = 0.8

MARGIN = 8
FACES = 6
MIB = 2**20


def lanes_of(shape):
    return lax.broadcasted_iota(jnp.int32, shape, len(shape) - 1)


def three_parts(value):
    high = value.astype(jnp.bfloat16)
    rest = value - high.astype(jnp.float32)
    middle = rest.astype(jnp.bfloat16)
    low = (rest - middle.astype(jnp.float32)).astype(jnp.bfloat16)
    return jnp.concatenate([high, middle, low], axis=-1)


def sum_parts(value):
    width = value.shape[-1] // 3
    return value[:, :width] + value[:, width : 2 * width] + value[:, 2 * width :]


def pick(onehot, value):
    return sum_parts(jnp.dot(onehot, three_parts(value), preferred_element_type=jnp.float32))


def spread(onehot, value):
    dims = (((0,), (0,)), ((), ()))
    return sum_parts(
        lax.dot_general(onehot, three_parts(value), dims, preferred_element_type=jnp.float32)
    )


def filled(ref, shape):
    return jnp.broadcast_to(ref[...], shape).astype(jnp.float32)


def is_even(axis):
    return lax.rem(lax.axis_index(axis), 2) == 0


def received(axis, one, two):
    even = is_even(axis)
    return jnp.where(even, two, one), jnp.where(even, one, two)


def fetch_all(copies):
    for copy in copies:
        copy.start()


def wait_all(copies):
    for copy in copies:
        copy.wait()


def pack_kernel(count_hbm, tiles_hbm, cells_hbm, out_ref, counts, tiles, cells, sems):
    owners_y, owners_x = counts.shape
    slots, lanes = tiles.shape[2], tiles.shape[3]
    pairs = [(count_hbm, counts), (cells_hbm, cells), (tiles_hbm, tiles)]
    copies = [pltpu.make_async_copy(a, b, sems.at[n]) for n, (a, b) in enumerate(pairs)]
    fetch_all(copies)
    wait_all(copies)
    lane = lanes_of((slots, lanes))
    slot = lax.broadcasted_iota(jnp.int32, (slots, lanes), 0)
    zero = jnp.zeros((slots, lanes), jnp.float32)
    for ox in range(owners_x):
        firsts, lasts, owns = [], [], []
        for oy in range(owners_y):
            owner = ox * owners_y + oy
            u = tiles[owner, 0]
            v = tiles[owner, 1]
            count = jnp.broadcast_to(counts[oy : oy + 1, ox : ox + 1], (slots, lanes))
            w = jnp.where(slot < count, tiles[owner, 2], 0.0)
            cell = jnp.broadcast_to(cells[oy, :, ox : ox + 1], (slots, lanes)).astype(jnp.float32)
            out_ref[owner, 0:slots] = u
            out_ref[owner, slots : 2 * slots] = v
            out_ref[owner, 2 * slots : 3 * slots] = w
            first = jnp.where(lane < 4, pltpu.roll(v, 2, 1), jnp.where(lane < 6, pltpu.roll(w, 4, 1), cell))
            firsts.append(jnp.where(lane < 2, u, first))
            last = jnp.where(
                lane >= lanes - 4,
                pltpu.roll(v, lanes - 2, 1),
                jnp.where(lane >= lanes - 6, pltpu.roll(w, lanes - 4, 1), cell),
            )
            lasts.append(jnp.where(lane >= lanes - 2, u, last))
            owns.append(cell)
        for oy in range(owners_y):
            after = firsts[oy + 1] if oy + 1 < owners_y else zero
            before = lasts[oy - 1] if oy > 0 else zero
            meta = jnp.where(lane < 16, after, jnp.where(lane >= lanes - 16, before, owns[oy]))
            out_ref[ox * owners_y + oy, 3 * slots : 4 * slots] = meta


def columns_kernel(ice_hbm, visc_hbm, fric_hbm, vel_hbm, one_ref, two_ref, ice, visc, fric, vel, sems):
    layers, rows, cols = visc_hbm.shape
    lanes = one_ref.shape[1]
    top = vel_hbm.at[:, vel_hbm.shape[1] - 1]
    pairs = [(ice_hbm, ice)]
    for side, span in enumerate((pl.ds(0, lanes), pl.ds(cols - lanes, lanes))):
        pairs.append((visc_hbm.at[:, :, span], visc.at[side]))
        pairs.append((fric_hbm.at[:, span], fric.at[side]))
        pairs.append((top.at[:, :, span], vel.at[side]))
    copies = [pltpu.make_async_copy(a, b, sems.at[n]) for n, (a, b) in enumerate(pairs)]
    fetch_all(copies)
    wait_all(copies)
    lane = lanes_of((rows, lanes))
    icefield = filled(ice, (rows, lanes))
    first = jnp.zeros((rows, lanes), jnp.float32)
    last = jnp.zeros((rows, lanes), jnp.float32)
    for k in range(layers + 4):
        if k < layers:
            mine = (visc[0, k], visc[1, k])
        elif k == layers:
            mine = (fric[0], fric[1])
        elif k == layers + 1:
            mine = (icefield, icefield)
        else:
            mine = (vel[0, k - layers - 2], vel[1, k - layers - 2])
        here = (lane >= 3 * k) & (lane < 3 * k + 3)
        first = jnp.where(here, pltpu.roll(mine[0], 3 * k, 1), first)
        there = (lane >= lanes - 3 - 3 * k) & (lane < lanes - 3 * k)
        last = jnp.where(there, pltpu.roll(mine[1], (lanes - 3 * k) % lanes, 1), last)
    even = is_even("gy")
    one_ref[...] = jnp.where(even, last, first)
    two_ref[...] = jnp.where(even, first, last)


def side_tile(before, after, k):
    lanes = before.shape[-1]
    lane = lanes_of(before.shape)
    left = pltpu.roll(before, (3 * k) % lanes, 1)
    right = pltpu.roll(after, (lanes - 3 * k) % lanes, 1)
    return jnp.where(lane < 3, right, jnp.where(lane >= lanes - 3, left, 0.0))


def ring_pair(load, tile, tiles):
    here = load(tile)
    lanes = here.shape[-1]
    lane = lanes_of(here.shape)
    before = pltpu.roll(jnp.where(lane == lanes - 1, load((tile - 1) % tiles), here), 1, 1)
    after = pltpu.roll(jnp.where(lane == 0, load((tile + 1) % tiles), here), lanes - 1, 1)
    return here, before, after


def factor_columns(layers, tile, tiles, load, store):
    gain = (0.5 * RELAX_WEIGHT) * load(layers + 1, tile, 0)
    up = None
    ratio = None
    for k in range(layers):
        here, south, north = ring_pair(lambda s: load(k, s, 0), tile, tiles)
        west = here + load(k, tile, -1)
        east = here + load(k, tile, 1)
        south = here + south
        north = here + north
        entry = 0.5 * (west + east + south + north)
        if k == 0:
            entry = entry + load(layers, tile, 0)
        if k > 0:
            entry = entry + (up - up * ratio)
        if k < layers - 1:
            above = (0.5 * VERTICAL_GAIN) * (here + load(k + 1, tile, 0))
            entry = entry + above
        inverse = jnp.where(entry > 0.0, 1.0 / entry, 0.0)
        scale = gain * inverse
        store(0, k, west * scale)
        store(1, k, east * scale)
        store(2, k, south * scale)
        store(3, k, north * scale)
        if k > 0:
            store(4, k, up * inverse)
        if k < layers - 1:
            up = above
            ratio = up * inverse
            store(5, k, ratio)
        else:
            store(4, 0, 2.0 * scale)


def first_columns(layers, rhs, coef, store):
    for n in range(2):
        value = rhs(n) * coef(4, 0)
        store(n, layers - 1, value)
        for k in range(layers - 2, -1, -1):
            value = coef(5, k) * value
            store(n, k, value)


def relax_columns(layers, tile, tiles, old, rhs, coef, store):
    forward = [[], []]
    for k in range(layers):
        west, east, south, north = (coef(f, k) for f in range(4))
        for n in range(2):
            here, before, after = ring_pair(lambda s: old(n, k, s, 0), tile, tiles)
            value = west * old(n, k, tile, -1) + east * old(n, k, tile, 1)
            value = value + (south * before + north * after)
            if k > 0:
                value = value + coef(4, k) * forward[n][k - 1]
            if k == layers - 1:
                value = value + rhs(n) * coef(4, 0)
            forward[n].append(value)
    for n in range(2):
        value = forward[n][layers - 1]
        for k in range(layers - 1, -1, -1):
            if k < layers - 1:
                value = forward[n][k] + coef(5, k) * value
            store(n, k, (1.0 - RELAX_WEIGHT) * old(n, k, tile, 0) + value)


def sources_kernel(
    slots, ice_hbm, tiles_ref, visc_hbm, fric_hbm, vel_hbm, one_any, two_any,
    rhs_ref, field, low_ref, high_ref, xone_ref, xtwo_ref, ice, vel, one, two, sems,
):
    layers, rows, cols = visc_hbm.shape
    lanes = tiles_ref.shape[1]
    owners = tiles_ref.shape[0] // (4 * slots)
    blocks = cols // lanes
    middle = pl.ds(MARGIN, rows)
    pairs = [(vel_hbm.at[:, layers - 1], vel), (one_any, one), (two_any, two), (ice_hbm, ice)]
    for t in range(blocks):
        span = pl.ds(t * lanes, lanes)
        pairs.append((visc_hbm.at[:, :, span], field.at[pl.ds(0, layers), t, middle, :]))
        pairs.append((fric_hbm.at[:, span], field.at[layers, t, middle, :]))
    copies = [pltpu.make_async_copy(a, b, sems.at[n]) for n, (a, b) in enumerate(pairs)]
    fetch_all(copies)
    edge = jnp.zeros((MARGIN, lanes), jnp.float32)
    for k in range(layers):
        for t in range(blocks + 1):
            field[k, t, 0:MARGIN] = edge
            field[k, t, MARGIN + rows : 2 * MARGIN + rows] = edge

    def channel(c):
        return jnp.concatenate(
            [tiles_ref[pl.ds(c * slots + s, owners, stride=4 * slots), :] for s in range(slots)], axis=0
        )

    seen_u, seen_v, weight, meta = channel(0), channel(1), channel(2), channel(3)
    count = owners * slots
    lane = lanes_of((count, lanes))
    row = lanes_of((count, rows))

    def onehot(column, b):
        cell = jnp.broadcast_to(column.astype(jnp.int32), (count, rows))
        return (cell == row * blocks + b).astype(jnp.bfloat16)

    even = is_even("gx")

    def send(k, t, low, high):
        xone_ref[k, t] = jnp.where(even, high, low)
        xtwo_ref[k, t] = jnp.where(even, low, high)

    def put(c, t, plane):
        rhs_ref[c, t] = plane
        send(layers + 2 + c, t, plane[0:4], plane[rows - 4 : rows])

    own = meta[:, lanes // 2 : lanes // 2 + 1]
    marks = jnp.concatenate([onehot(own, b) for b in range(blocks)], axis=1)
    wait_all(copies[:1])
    surface = jnp.concatenate(
        [
            jnp.concatenate([vel[c, :, b * lanes : (b + 1) * lanes] for b in range(blocks)], axis=0)
            for c in range(2)
        ],
        axis=1,
    )
    weights = jnp.concatenate([weight, weight], axis=1)
    terms = weights * (pick(marks, surface) - jnp.concatenate([seen_u, seen_v], axis=1))
    total = spread(marks, terms)
    for c in range(2):
        for b in range(blocks):
            put(c, b, total[b * rows : (b + 1) * rows, c * lanes : (c + 1) * lanes])

    wait_all(copies[1:4])
    icefield = filled(ice, (rows, lanes))
    from_before, from_after = received("gy", one[...], two[...])
    for k in range(layers + 2):
        field[k, blocks, middle] = side_tile(from_before, from_after, k)
        for t in range(blocks):
            if k == layers + 1:
                field[k, t, middle] = icefield
    beside = jnp.concatenate(
        [side_tile(from_before, from_after, layers + 2 + c) for c in range(2)], axis=1
    )
    mark_after = onehot(meta[:, 8:9], 0)
    mark_before = onehot(meta[:, lanes - 8 : lanes - 7], blocks - 1)
    weight_after = jnp.where(lane < 2, pltpu.roll(meta, lanes - 4, 1), 0.0)
    weight_before = jnp.where(lane >= lanes - 2, pltpu.roll(meta, 4, 1), 0.0)
    after = jnp.concatenate([meta, pltpu.roll(meta, lanes - 2, 1)], axis=1)
    before = jnp.concatenate([meta, pltpu.roll(meta, 2, 1)], axis=1)
    terms_after = jnp.concatenate([weight_after] * 2, axis=1) * (pick(mark_after, beside) - after)
    terms_before = jnp.concatenate([weight_before] * 2, axis=1) * (pick(mark_before, beside) - before)
    side = spread(mark_after, terms_after) + spread(mark_before, terms_before)
    for c in range(2):
        put(c, blocks, side[:, c * lanes : (c + 1) * lanes])

    wait_all(copies[4:])
    for k in range(layers + 2):
        for t in range(blocks + 1):
            low = field[k, t, MARGIN : MARGIN + 8]
            high = field[k, t, MARGIN + rows - 8 : MARGIN + rows]
            low_ref[k, t] = low
            high_ref[k, t] = high
            send(k, t, low[0:4], high[4:8])


def inner_kernel(field, rhs, adj_hbm, low_ref, high_ref, base_ref, coef, one, two, three, sem_out):
    steps, tiles, _, layers, _, lanes = coef.shape
    rows = three.shape[3]
    def factors(r, carry):
        for t in range(tiles):

            def load(k, s, move):
                return field[k, s, pl.ds(MARGIN + r + move, 8, stride=steps), :]

            def store(f, k, value):
                coef[r, t, f, k] = value

            factor_columns(layers, t, tiles, load, store)
        return carry

    lax.fori_loop(0, steps, factors, 0, unroll=3)

    sublane = lax.broadcasted_iota(jnp.int32, (8, lanes), 0)

    def wrap(ref):
        for n in range(2):
            for k in range(layers):
                for t in range(tiles):
                    last = pltpu.roll(ref[n, k, t, steps], 1, 0)
                    ref[n, k, t, 0] = jnp.where(sublane == 0, 0.0, last)
                    first = pltpu.roll(ref[n, k, t, 1], 7, 0)
                    ref[n, k, t, steps + 1] = jnp.where(sublane == 7, 0.0, first)

    def rhs_of(r, t):
        return lambda n: rhs[n, t, pl.ds(r, 8, stride=steps), :]

    def coef_of(r, t):
        return lambda f, k: coef[r, t, f, k]

    def first_sweep(r, carry):
        for t in range(tiles):

            def store(n, k, value):
                one[n, k, t, r + 1] = value

            first_columns(layers, rhs_of(r, t), coef_of(r, t), store)
        return carry

    lax.fori_loop(0, steps, first_sweep, 0, unroll=2)
    wrap(one)

    def second_sweep(r, carry):
        for t in range(tiles):

            def old(n, k, s, move):
                return one[n, k, s, r + 1 + move]

            def store(n, k, value):
                two[n, k, t, r + 1] = value

            relax_columns(layers, t, tiles, old, rhs_of(r, t), coef_of(r, t), store)
        return carry

    lax.fori_loop(0, steps, second_sweep, 0, unroll=4)
    wrap(two)

    def result(t):
        middle = pl.ds(8, rows - 16)
        span = pl.ds(t * lanes, lanes)
        return pltpu.make_async_copy(three.at[:, :, t, middle, :], adj_hbm.at[:, :, middle, span], sem_out.at[t])

    for t in range(tiles - 1):

        def third_sweep(r, carry):
            def old(n, k, s, move):
                return two[n, k, s, r + 1 + move]

            def store(n, k, value):
                three[n, k, t, pl.ds(r, 8, stride=steps), :] = value

            relax_columns(layers, t, tiles, old, rhs_of(r, t), coef_of(r, t), store)
            return carry

        lax.fori_loop(0, steps, third_sweep, 0, unroll=12)
        result(t).start()
        for n in range(2):
            for k in range(layers):
                low_ref[n, k, t] = three[n, k, t, 0:8]
                high_ref[n, k, t] = three[n, k, t, rows - 8 : rows]
        for n in range(2):
            base_ref[n, :, t * lanes : (t + 1) * lanes] = three[n, 0, t]
    for t in range(tiles - 1):
        result(t).wait()


def edges_kernel(
    ice_hbm, own_low, own_high, one_ref, two_ref, rhs_ref, low_ref, high_ref, base_ref, vel_hbm, adj_in,
    adj_hbm, grad_hbm, ice, field, coefs, rhs, one, two, patch, vel, grad, sem_in, sem_out,
):
    tiles, _, layers = coefs.shape[1:4]
    rows, cols = grad.shape
    lanes = coefs.shape[5]
    blocks = tiles - 1
    spans = [pl.ds(0, 8), pl.ds(rows - 8, 8), pl.ds(8, rows - 16)]
    gradients = [
        pltpu.make_async_copy(grad.at[span, :], grad_hbm.at[span, :], sem_out.at[2 + n])
        for n, span in enumerate(spans)
    ]
    fetches = [
        pltpu.make_async_copy(vel_hbm.at[:, 0], vel, sem_in.at[0]),
        pltpu.make_async_copy(ice_hbm, ice, sem_in.at[1]),
    ]
    fetch_all(fetches)
    for k in range(layers + 4):
        for t in range(tiles):
            before, after = received("gx", one_ref[k, t], two_ref[k, t])
            if k < layers + 2:
                field[0, k, t, 0:4] = before
                field[0, k, t, 4:12] = own_low[k, t]
                field[1, k, t, 4:12] = own_high[k, t]
                field[1, k, t, 12:16] = after
            else:
                n = k - layers - 2
                rhs[0, n, t, 0:4] = before
                rhs[0, n, t, 4:12] = rhs_ref[n, t, 0:8]
                rhs[1, n, t, 4:12] = rhs_ref[n, t, rows - 8 : rows]
                rhs[1, n, t, 12:16] = after
    wait_all(fetches)
    inside = spans[2]
    product = base_ref[0, inside] * vel[0, inside] + base_ref[1, inside] * vel[1, inside]
    grad[inside] = -filled(ice, (rows - 16, cols)) * product
    gradients[2].start()
    starts = (2, 6)

    def at(ref, start):
        return lambda *index: ref[(*index, pl.ds(start, 8), slice(None))]

    for t in range(tiles):
        for side in range(2):

            def load(k, s, move):
                return field[side, k, s, pl.ds(starts[side] + move, 8), :]

            def store(f, k, value):
                coefs[side, t, f, k, pl.ds(starts[side], 8), :] = value

            factor_columns(layers, t, tiles, load, store)

    def sides(t, start, side):
        def rhs_of(n):
            return rhs[side, n, t, pl.ds(start, 8), :]

        def coef(f, k):
            return coefs[side, t, f, k, pl.ds(start, 8), :]

        return rhs_of, coef

    for t in range(tiles):
        for side in range(2):
            rhs_of, coef = sides(t, starts[side], side)

            def store(n, k, value):
                one[side, n, k, t, pl.ds(starts[side], 8), :] = value

            first_columns(layers, rhs_of, coef, store)
    for t in range(tiles):
        for side in range(2):
            rhs_of, coef = sides(t, starts[side], side)

            def old(n, k, s, move):
                return one[side, n, k, s, pl.ds(starts[side] + move, 8), :]

            def store(n, k, value):
                two[side, n, k, t, pl.ds(starts[side], 8), :] = value

            relax_columns(layers, t, tiles, old, rhs_of, coef, store)

    def result(side):
        return pltpu.make_async_copy(
            patch.at[side], adj_hbm.at[:, :, pl.ds(side * (rows - 8), 8), :], sem_out.at[side]
        )

    sublane = lax.broadcasted_iota(jnp.int32, (8, lanes), 0)
    wrong = (sublane < 3, sublane >= 5)
    inner = (low_ref, high_ref)
    for side in range(2):
        for t in range(blocks):
            rhs_of, coef = sides(t, 4, side)
            span = slice(t * lanes, (t + 1) * lanes)

            def old(n, k, s, move):
                return two[side, n, k, s, pl.ds(4 + move, 8), :]

            def store(n, k, value):
                patch[side, n, k, :, span] = jnp.where(wrong[side], value, inner[side][n, k, t])

            relax_columns(layers, t, tiles, old, rhs_of, coef, store)
        result(side).start()
    for side in range(2):
        product = patch[side, 0, 0] * vel[0, spans[side]] + patch[side, 1, 0] * vel[1, spans[side]]
        grad[spans[side]] = -filled(ice, (8, cols)) * product
        gradients[side].start()
    wait_all(gradients)
    for side in range(2):
        result(side).wait()


def whole(space=pltpu.VMEM):
    return pl.BlockSpec(memory_space=space)


def per_device(velocity, viscosity, friction, ice_mask, obs_tiles, obs_cell, obs_count):
    layers, rows, cols = viscosity.shape
    owners_x, owners_y, slots, channels, lanes = obs_tiles.shape[2:]
    blocks = cols // lanes
    tiles = blocks + 1
    owners = owners_x * owners_y
    steps = rows // 8
    f32 = jnp.float32

    def shape(*dims):
        return jax.ShapeDtypeStruct(dims, f32)

    def grant(mib):
        return pltpu.CompilerParams(vmem_limit_bytes=int(mib * MIB))

    def swap(value, axis, first):
        pairs = []
        for i in range(first, lax.axis_size(axis) - 1, 2):
            pairs += [(i, i + 1), (i + 1, i)]
        return lax.ppermute(value, axis, pairs)

    tiles_in = jnp.transpose(obs_tiles.reshape(owners, slots, channels, lanes), (0, 2, 1, 3))
    cells_in = jnp.transpose(obs_cell[0, 0], (1, 2, 0))
    counts_in = jnp.transpose(obs_count[0, 0], (1, 0))
    def part(dims, *index):
        return pl.BlockSpec(dims, lambda i: index)

    i32 = jnp.int32
    plane = shape(rows, lanes)
    hbm = whole(pltpu.HBM)
    anywhere = whole(pl.ANY)
    packed = pl.pallas_call(
        pack_kernel,
        out_shape=shape(owners, 4 * slots, lanes),
        in_specs=[hbm] * 3,
        out_specs=whole(),
        scratch_shapes=[
            pltpu.VMEM(counts_in.shape, i32),
            pltpu.VMEM(tiles_in.shape, f32),
            pltpu.VMEM(cells_in.shape, i32),
            pltpu.SemaphoreType.DMA((3,)),
        ],
        compiler_params=grant(61.5),
        cost_estimate=pl.CostEstimate(flops=4 * 10**9, transcendentals=0, bytes_accessed=0),
        name="pack",
    )(counts_in, tiles_in, cells_in)
    arrived = lax.all_to_all(packed, ("gx", "gy"), split_axis=0, concat_axis=0, tiled=True)
    ysend_one, ysend_two = pl.pallas_call(
        columns_kernel,
        out_shape=(plane, plane),
        in_specs=[hbm] * 4,
        out_specs=(whole(), whole()),
        scratch_shapes=[
            pltpu.VMEM((1, 1), i32),
            pltpu.VMEM((2, layers, rows, lanes), f32),
            pltpu.VMEM((2, rows, lanes), f32),
            pltpu.VMEM((2, 2, rows, lanes), f32),
            pltpu.SemaphoreType.DMA((7,)),
        ],
        compiler_params=grant(61.5),
        cost_estimate=pl.CostEstimate(flops=4 * 10**9, transcendentals=0, bytes_accessed=0),
        name="columns",
    )(ice_mask, viscosity, friction, velocity)
    yone = swap(ysend_one, "gy", 0)
    ytwo = swap(ysend_two, "gy", 1)

    own = shape(layers + 2, tiles, 8, lanes)
    edge = shape(layers + 4, tiles, 4, lanes)
    rhs, field, own_low, own_high, xsend_one, xsend_two = pl.pallas_call(
        functools.partial(sources_kernel, slots),
        out_shape=(
            shape(2, tiles, rows, lanes),
            shape(layers + 2, tiles, rows + 2 * MARGIN, lanes),
            own,
            own,
            edge,
            edge,
        ),
        in_specs=[hbm, whole(), hbm, hbm, hbm, anywhere, anywhere],
        out_specs=(whole(),) * 6,
        scratch_shapes=[
            pltpu.VMEM((1, 1), i32),
            pltpu.VMEM((2, rows, cols), f32),
            pltpu.VMEM((rows, lanes), f32),
            pltpu.VMEM((rows, lanes), f32),
            pltpu.SemaphoreType.DMA((2 * blocks + 4,)),
        ],
        compiler_params=grant(47.5),
        cost_estimate=pl.CostEstimate(flops=4 * 10**9, transcendentals=0, bytes_accessed=0),
        name="sources",
    )(
        ice_mask, arrived.reshape(owners * 4 * slots, lanes), viscosity, friction, velocity, yone, ytwo
    )
    xone = swap(xsend_one, "gx", 0)
    xtwo = swap(xsend_two, "gx", 1)

    ends = shape(2, layers, blocks, 8, lanes)
    wide = pltpu.VMEM((2, layers, tiles, steps + 2, 8, lanes), f32)
    adjoint, low, high, base = pl.pallas_call(
        inner_kernel,
        out_shape=(shape(*velocity.shape), ends, ends, shape(2, rows, cols)),
        in_specs=[whole(), whole()],
        out_specs=(hbm, whole(), whole(), whole()),
        scratch_shapes=[
            pltpu.VMEM((steps, tiles, FACES, layers, 8, lanes), f32),
            wide,
            wide,
            pltpu.VMEM((2, layers, blocks, rows, lanes), f32),
            pltpu.SemaphoreType.DMA((blocks,)),
        ],
        compiler_params=grant(28),
        cost_estimate=pl.CostEstimate(flops=4 * 10**9, transcendentals=0, bytes_accessed=0),
        name="inner",
    )(field, rhs)

    return pl.pallas_call(
        edges_kernel,
        out_shape=(shape(*velocity.shape), shape(rows, cols)),
        in_specs=[hbm] + [whole()] * 8 + [hbm, hbm],
        out_specs=(hbm, hbm),
        scratch_shapes=[
            pltpu.VMEM((1, 1), i32),
            pltpu.VMEM((2, layers + 2, tiles, 16, lanes), f32),
            pltpu.VMEM((2, tiles, FACES, layers, 16, lanes), f32),
            pltpu.VMEM((2, 2, tiles, 16, lanes), f32),
            pltpu.VMEM((2, 2, layers, tiles, 16, lanes), f32),
            pltpu.VMEM((2, 2, layers, tiles, 16, lanes), f32),
            pltpu.VMEM((2, 2, layers, 8, cols), f32),
            pltpu.VMEM((2, rows, cols), f32),
            pltpu.VMEM((rows, cols), f32),
            pltpu.SemaphoreType.DMA((2,)),
            pltpu.SemaphoreType.DMA((5,)),
        ],
        input_output_aliases={10: 0},
        compiler_params=grant(14),
        cost_estimate=pl.CostEstimate(flops=4 * 10**9, transcendentals=0, bytes_accessed=0),
        name="edges",
    )(ice_mask, own_low, own_high, xone, xtwo, rhs, low, high, base, velocity, adjoint)


def solution(mesh):
    placed = (
        P(None, None, "gx", "gy"),
        P(None, "gx", "gy"),
        P("gx", "gy"),
        P("gx", "gy"),
        P("gx", "gy", None, None, None, None, None),
        P("gx", "gy", None, None, None),
        P("gx", "gy", None, None),
    )
    return jax.shard_map(
        per_device,
        mesh=mesh,
        in_specs=placed,
        out_specs=(P(None, None, "gx", "gy"), P("gx", "gy")),
        check_vma=False,
    )
```

```python
import functools

import jax
import jax.numpy as jnp
from jax import lax
from jax.experimental import pallas as pl
from jax.experimental.pallas import tpu as pltpu
from jax.sharding import PartitionSpec as P

VERTICAL_GAIN = 2.0
RELAX_WEIGHT = 0.8

MARGIN = 8
FACES = 6
MIB = 2**20


def lanes_of(shape):
    return lax.broadcasted_iota(jnp.int32, shape, len(shape) - 1)


def three_parts(value):
    high = value.astype(jnp.bfloat16)
    rest = value - high.astype(jnp.float32)
    middle = rest.astype(jnp.bfloat16)
    low = (rest - middle.astype(jnp.float32)).astype(jnp.bfloat16)
    return jnp.concatenate([high, middle, low], axis=-1)


def sum_parts(value):
    width = value.shape[-1] // 3
    return value[:, :width] + value[:, width : 2 * width] + value[:, 2 * width :]


def pick(onehot, value):
    return sum_parts(jnp.dot(onehot, three_parts(value), preferred_element_type=jnp.float32))


def spread(onehot, value):
    dims = (((0,), (0,)), ((), ()))
    return sum_parts(
        lax.dot_general(onehot, three_parts(value), dims, preferred_element_type=jnp.float32)
    )


def filled(ref, shape):
    return jnp.broadcast_to(ref[...], shape).astype(jnp.float32)


def is_even(axis):
    return lax.rem(lax.axis_index(axis), 2) == 0


def received(axis, one, two):
    even = is_even(axis)
    return jnp.where(even, two, one), jnp.where(even, one, two)


def fetch_all(copies):
    for copy in copies:
        copy.start()


def wait_all(copies):
    for copy in copies:
        copy.wait()


def pack_kernel(count_hbm, tiles_hbm, cells_hbm, out_ref, counts, tiles, cells, sems):
    owners_y, owners_x = counts.shape
    slots, lanes = tiles.shape[2], tiles.shape[3]
    pairs = [(count_hbm, counts), (cells_hbm, cells), (tiles_hbm, tiles)]
    copies = [pltpu.make_async_copy(a, b, sems.at[n]) for n, (a, b) in enumerate(pairs)]
    fetch_all(copies)
    wait_all(copies)
    lane = lanes_of((slots, lanes))
    slot = lax.broadcasted_iota(jnp.int32, (slots, lanes), 0)
    zero = jnp.zeros((slots, lanes), jnp.float32)
    for ox in range(owners_x):
        firsts, lasts, owns = [], [], []
        for oy in range(owners_y):
            owner = ox * owners_y + oy
            u = tiles[owner, 0]
            v = tiles[owner, 1]
            count = jnp.broadcast_to(counts[oy : oy + 1, ox : ox + 1], (slots, lanes))
            w = jnp.where(slot < count, tiles[owner, 2], 0.0)
            cell = jnp.broadcast_to(cells[oy, :, ox : ox + 1], (slots, lanes)).astype(jnp.float32)
            out_ref[owner, 0:slots] = u
            out_ref[owner, slots : 2 * slots] = v
            out_ref[owner, 2 * slots : 3 * slots] = w
            first = jnp.where(lane < 4, pltpu.roll(v, 2, 1), jnp.where(lane < 6, pltpu.roll(w, 4, 1), cell))
            firsts.append(jnp.where(lane < 2, u, first))
            last = jnp.where(
                lane >= lanes - 4,
                pltpu.roll(v, lanes - 2, 1),
                jnp.where(lane >= lanes - 6, pltpu.roll(w, lanes - 4, 1), cell),
            )
            lasts.append(jnp.where(lane >= lanes - 2, u, last))
            owns.append(cell)
        for oy in range(owners_y):
            after = firsts[oy + 1] if oy + 1 < owners_y else zero
            before = lasts[oy - 1] if oy > 0 else zero
            meta = jnp.where(lane < 16, after, jnp.where(lane >= lanes - 16, before, owns[oy]))
            out_ref[ox * owners_y + oy, 3 * slots : 4 * slots] = meta


def columns_kernel(ice_hbm, visc_ref, fric_ref, top_ref, one_ref, two_ref, ice, sem):
    layers, rows, cols = visc_ref.shape
    lanes = one_ref.shape[1]
    copy = pltpu.make_async_copy(ice_hbm, ice, sem)
    copy.start()
    copy.wait()
    left, right = slice(0, lanes), slice(cols - lanes, cols)
    lane = lanes_of((rows, lanes))
    icefield = filled(ice, (rows, lanes))
    first = jnp.zeros((rows, lanes), jnp.float32)
    last = jnp.zeros((rows, lanes), jnp.float32)
    for k in range(layers + 4):
        if k < layers:
            mine = (visc_ref[k, :, left], visc_ref[k, :, right])
        elif k == layers:
            mine = (fric_ref[:, left], fric_ref[:, right])
        elif k == layers + 1:
            mine = (icefield, icefield)
        else:
            mine = (top_ref[k - layers - 2, :, left], top_ref[k - layers - 2, :, right])
        here = (lane >= 3 * k) & (lane < 3 * k + 3)
        first = jnp.where(here, pltpu.roll(mine[0], 3 * k, 1), first)
        there = (lane >= lanes - 3 - 3 * k) & (lane < lanes - 3 * k)
        last = jnp.where(there, pltpu.roll(mine[1], (lanes - 3 * k) % lanes, 1), last)
    even = is_even("gy")
    one_ref[...] = jnp.where(even, last, first)
    two_ref[...] = jnp.where(even, first, last)


def side_tile(before, after, k):
    lanes = before.shape[-1]
    lane = lanes_of(before.shape)
    left = pltpu.roll(before, (3 * k) % lanes, 1)
    right = pltpu.roll(after, (lanes - 3 * k) % lanes, 1)
    return jnp.where(lane < 3, right, jnp.where(lane >= lanes - 3, left, 0.0))


def ring_pair(load, tile, tiles):
    here = load(tile)
    lanes = here.shape[-1]
    lane = lanes_of(here.shape)
    before = pltpu.roll(jnp.where(lane == lanes - 1, load((tile - 1) % tiles), here), 1, 1)
    after = pltpu.roll(jnp.where(lane == 0, load((tile + 1) % tiles), here), lanes - 1, 1)
    return here, before, after


def factor_columns(layers, tile, tiles, load, store):
    gain = (0.5 * RELAX_WEIGHT) * load(layers + 1, tile, 0)
    up = None
    ratio = None
    for k in range(layers):
        here, south, north = ring_pair(lambda s: load(k, s, 0), tile, tiles)
        west = here + load(k, tile, -1)
        east = here + load(k, tile, 1)
        south = here + south
        north = here + north
        entry = 0.5 * (west + east + south + north)
        if k == 0:
            entry = entry + load(layers, tile, 0)
        if k > 0:
            entry = entry + (up - up * ratio)
        if k < layers - 1:
            above = (0.5 * VERTICAL_GAIN) * (here + load(k + 1, tile, 0))
            entry = entry + above
        inverse = jnp.where(entry > 0.0, 1.0 / entry, 0.0)
        scale = gain * inverse
        store(0, k, west * scale)
        store(1, k, east * scale)
        store(2, k, south * scale)
        store(3, k, north * scale)
        if k > 0:
            store(4, k, up * inverse)
        if k < layers - 1:
            up = above
            ratio = up * inverse
            store(5, k, ratio)
        else:
            store(4, 0, 2.0 * scale)


def first_columns(layers, rhs, coef, store):
    for n in range(2):
        value = rhs(n) * coef(4, 0)
        store(n, layers - 1, value)
        for k in range(layers - 2, -1, -1):
            value = coef(5, k) * value
            store(n, k, value)


def relax_columns(layers, tile, tiles, old, rhs, coef, store):
    forward = [[], []]
    for k in range(layers):
        west, east, south, north = (coef(f, k) for f in range(4))
        for n in range(2):
            here, before, after = ring_pair(lambda s: old(n, k, s, 0), tile, tiles)
            value = west * old(n, k, tile, -1) + east * old(n, k, tile, 1)
            value = value + (south * before + north * after)
            if k > 0:
                value = value + coef(4, k) * forward[n][k - 1]
            if k == layers - 1:
                value = value + rhs(n) * coef(4, 0)
            forward[n].append(value)
    for n in range(2):
        value = forward[n][layers - 1]
        for k in range(layers - 1, -1, -1):
            if k < layers - 1:
                value = forward[n][k] + coef(5, k) * value
            store(n, k, (1.0 - RELAX_WEIGHT) * old(n, k, tile, 0) + value)


def sources_kernel(
    slots, ice_hbm, tiles_ref, visc_hbm, fric_hbm, vel, one, two,
    rhs_ref, field, low_ref, high_ref, xone_ref, xtwo_ref, ice, sems,
):
    layers, rows, cols = visc_hbm.shape
    lanes = tiles_ref.shape[1]
    owners = tiles_ref.shape[0] // (4 * slots)
    blocks = cols // lanes
    middle = pl.ds(MARGIN, rows)
    pairs = [(ice_hbm, ice)]
    for t in range(blocks):
        span = pl.ds(t * lanes, lanes)
        pairs.append((visc_hbm.at[:, :, span], field.at[pl.ds(0, layers), t, middle, :]))
        pairs.append((fric_hbm.at[:, span], field.at[layers, t, middle, :]))
    copies = [pltpu.make_async_copy(a, b, sems.at[n]) for n, (a, b) in enumerate(pairs)]
    fetch_all(copies)
    edge = jnp.zeros((MARGIN, lanes), jnp.float32)
    for k in range(layers):
        for t in range(blocks + 1):
            field[k, t, 0:MARGIN] = edge
            field[k, t, MARGIN + rows : 2 * MARGIN + rows] = edge

    def channel(c):
        return jnp.concatenate(
            [tiles_ref[pl.ds(c * slots + s, owners, stride=4 * slots), :] for s in range(slots)], axis=0
        )

    seen_u, seen_v, weight, meta = channel(0), channel(1), channel(2), channel(3)
    count = owners * slots
    lane = lanes_of((count, lanes))
    row = lanes_of((count, rows))

    def onehot(column, b):
        cell = jnp.broadcast_to(column.astype(jnp.int32), (count, rows))
        return (cell == row * blocks + b).astype(jnp.bfloat16)

    even = is_even("gx")

    def send(k, t, low, high):
        xone_ref[k, t] = jnp.where(even, high, low)
        xtwo_ref[k, t] = jnp.where(even, low, high)

    def put(c, t, plane):
        rhs_ref[c, t] = plane
        send(layers + 2 + c, t, plane[0:4], plane[rows - 4 : rows])

    own = meta[:, lanes // 2 : lanes // 2 + 1]
    marks = jnp.concatenate([onehot(own, b) for b in range(blocks)], axis=1)
    surface = jnp.concatenate(
        [
            jnp.concatenate([vel[c, :, b * lanes : (b + 1) * lanes] for b in range(blocks)], axis=0)
            for c in range(2)
        ],
        axis=1,
    )
    weights = jnp.concatenate([weight, weight], axis=1)
    terms = weights * (pick(marks, surface) - jnp.concatenate([seen_u, seen_v], axis=1))
    total = spread(marks, terms)
    for c in range(2):
        for b in range(blocks):
            put(c, b, total[b * rows : (b + 1) * rows, c * lanes : (c + 1) * lanes])

    wait_all(copies[:1])
    icefield = filled(ice, (rows, lanes))
    from_before, from_after = received("gy", one[...], two[...])
    for k in range(layers + 2):
        field[k, blocks, middle] = side_tile(from_before, from_after, k)
        for t in range(blocks):
            if k == layers + 1:
                field[k, t, middle] = icefield
    beside = jnp.concatenate(
        [side_tile(from_before, from_after, layers + 2 + c) for c in range(2)], axis=1
    )
    mark_after = onehot(meta[:, 8:9], 0)
    mark_before = onehot(meta[:, lanes - 8 : lanes - 7], blocks - 1)
    weight_after = jnp.where(lane < 2, pltpu.roll(meta, lanes - 4, 1), 0.0)
    weight_before = jnp.where(lane >= lanes - 2, pltpu.roll(meta, 4, 1), 0.0)
    after = jnp.concatenate([meta, pltpu.roll(meta, lanes - 2, 1)], axis=1)
    before = jnp.concatenate([meta, pltpu.roll(meta, 2, 1)], axis=1)
    terms_after = jnp.concatenate([weight_after] * 2, axis=1) * (pick(mark_after, beside) - after)
    terms_before = jnp.concatenate([weight_before] * 2, axis=1) * (pick(mark_before, beside) - before)
    side = spread(mark_after, terms_after) + spread(mark_before, terms_before)
    for c in range(2):
        put(c, blocks, side[:, c * lanes : (c + 1) * lanes])

    wait_all(copies[1:])
    for k in range(layers + 2):
        for t in range(blocks + 1):
            low = field[k, t, MARGIN : MARGIN + 8]
            high = field[k, t, MARGIN + rows - 8 : MARGIN + rows]
            low_ref[k, t] = low
            high_ref[k, t] = high
            send(k, t, low[0:4], high[4:8])


def inner_kernel(field, rhs, adj_hbm, low_ref, high_ref, base_ref, coef, one, two, three, sem_out):
    steps, tiles, _, layers, _, lanes = coef.shape
    rows = three.shape[3]
    def factors(r, carry):
        for t in range(tiles):

            def load(k, s, move):
                return field[k, s, pl.ds(MARGIN + r + move, 8, stride=steps), :]

            def store(f, k, value):
                coef[r, t, f, k] = value

            factor_columns(layers, t, tiles, load, store)
        return carry

    lax.fori_loop(0, steps, factors, 0, unroll=3)

    sublane = lax.broadcasted_iota(jnp.int32, (8, lanes), 0)

    def wrap(ref):
        for n in range(2):
            for k in range(layers):
                for t in range(tiles):
                    last = pltpu.roll(ref[n, k, t, steps], 1, 0)
                    ref[n, k, t, 0] = jnp.where(sublane == 0, 0.0, last)
                    first = pltpu.roll(ref[n, k, t, 1], 7, 0)
                    ref[n, k, t, steps + 1] = jnp.where(sublane == 7, 0.0, first)

    def rhs_of(r, t):
        return lambda n: rhs[n, t, pl.ds(r, 8, stride=steps), :]

    def coef_of(r, t):
        return lambda f, k: coef[r, t, f, k]

    def first_sweep(r, carry):
        for t in range(tiles):

            def store(n, k, value):
                one[n, k, t, r + 1] = value

            first_columns(layers, rhs_of(r, t), coef_of(r, t), store)
        return carry

    lax.fori_loop(0, steps, first_sweep, 0, unroll=2)
    wrap(one)

    def second_sweep(r, carry):
        for t in range(tiles):

            def old(n, k, s, move):
                return one[n, k, s, r + 1 + move]

            def store(n, k, value):
                two[n, k, t, r + 1] = value

            relax_columns(layers, t, tiles, old, rhs_of(r, t), coef_of(r, t), store)
        return carry

    lax.fori_loop(0, steps, second_sweep, 0, unroll=4)
    wrap(two)

    def result(t):
        middle = pl.ds(8, rows - 16)
        span = pl.ds(t * lanes, lanes)
        return pltpu.make_async_copy(three.at[:, :, t, middle, :], adj_hbm.at[:, :, middle, span], sem_out.at[t])

    for t in range(tiles - 1):

        def third_sweep(r, carry):
            def old(n, k, s, move):
                return two[n, k, s, r + 1 + move]

            def store(n, k, value):
                three[n, k, t, pl.ds(r, 8, stride=steps), :] = value

            relax_columns(layers, t, tiles, old, rhs_of(r, t), coef_of(r, t), store)
            return carry

        lax.fori_loop(0, steps, third_sweep, 0, unroll=12)
        result(t).start()
        for n in range(2):
            for k in range(layers):
                low_ref[n, k, t] = three[n, k, t, 0:8]
                high_ref[n, k, t] = three[n, k, t, rows - 8 : rows]
        for n in range(2):
            base_ref[n, :, t * lanes : (t + 1) * lanes] = three[n, 0, t]
    for t in range(tiles - 1):
        result(t).wait()


def edges_kernel(
    ice_hbm, own_low, own_high, one_ref, two_ref, rhs_ref, low_ref, high_ref, base_ref, vel_hbm, adj_in,
    adj_hbm, grad_hbm, ice, field, coefs, rhs, one, two, patch, vel, grad, sem_in, sem_out,
):
    tiles, _, layers = coefs.shape[1:4]
    rows, cols = grad.shape
    lanes = coefs.shape[5]
    blocks = tiles - 1
    spans = [pl.ds(0, 8), pl.ds(rows - 8, 8), pl.ds(8, rows - 16)]
    gradients = [
        pltpu.make_async_copy(grad.at[span, :], grad_hbm.at[span, :], sem_out.at[2 + n])
        for n, span in enumerate(spans)
    ]
    fetches = [
        pltpu.make_async_copy(vel_hbm.at[:, 0], vel, sem_in.at[0]),
        pltpu.make_async_copy(ice_hbm, ice, sem_in.at[1]),
    ]
    fetch_all(fetches)
    for k in range(layers + 4):
        for t in range(tiles):
            before, after = received("gx", one_ref[k, t], two_ref[k, t])
            if k < layers + 2:
                field[0, k, t, 0:4] = before
                field[0, k, t, 4:12] = own_low[k, t]
                field[1, k, t, 4:12] = own_high[k, t]
                field[1, k, t, 12:16] = after
            else:
                n = k - layers - 2
                rhs[0, n, t, 0:4] = before
                rhs[0, n, t, 4:12] = rhs_ref[n, t, 0:8]
                rhs[1, n, t, 4:12] = rhs_ref[n, t, rows - 8 : rows]
                rhs[1, n, t, 12:16] = after
    wait_all(fetches)
    inside = spans[2]
    product = base_ref[0, inside] * vel[0, inside] + base_ref[1, inside] * vel[1, inside]
    grad[inside] = -filled(ice, (rows - 16, cols)) * product
    gradients[2].start()
    starts = (2, 6)

    def at(ref, start):
        return lambda *index: ref[(*index, pl.ds(start, 8), slice(None))]

    for t in range(tiles):
        for side in range(2):

            def load(k, s, move):
                return field[side, k, s, pl.ds(starts[side] + move, 8), :]

            def store(f, k, value):
                coefs[side, t, f, k, pl.ds(starts[side], 8), :] = value

            factor_columns(layers, t, tiles, load, store)

    def sides(t, start, side):
        def rhs_of(n):
            return rhs[side, n, t, pl.ds(start, 8), :]

        def coef(f, k):
            return coefs[side, t, f, k, pl.ds(start, 8), :]

        return rhs_of, coef

    for t in range(tiles):
        for side in range(2):
            rhs_of, coef = sides(t, starts[side], side)

            def store(n, k, value):
                one[side, n, k, t, pl.ds(starts[side], 8), :] = value

            first_columns(layers, rhs_of, coef, store)
    for t in range(tiles):
        for side in range(2):
            rhs_of, coef = sides(t, starts[side], side)

            def old(n, k, s, move):
                return one[side, n, k, s, pl.ds(starts[side] + move, 8), :]

            def store(n, k, value):
                two[side, n, k, t, pl.ds(starts[side], 8), :] = value

            relax_columns(layers, t, tiles, old, rhs_of, coef, store)

    def result(side):
        return pltpu.make_async_copy(
            patch.at[side], adj_hbm.at[:, :, pl.ds(side * (rows - 8), 8), :], sem_out.at[side]
        )

    sublane = lax.broadcasted_iota(jnp.int32, (8, lanes), 0)
    wrong = (sublane < 3, sublane >= 5)
    inner = (low_ref, high_ref)
    for side in range(2):
        for t in range(blocks):
            rhs_of, coef = sides(t, 4, side)
            span = slice(t * lanes, (t + 1) * lanes)

            def old(n, k, s, move):
                return two[side, n, k, s, pl.ds(4 + move, 8), :]

            def store(n, k, value):
                patch[side, n, k, :, span] = jnp.where(wrong[side], value, inner[side][n, k, t])

            relax_columns(layers, t, tiles, old, rhs_of, coef, store)
        result(side).start()
    for side in range(2):
        product = patch[side, 0, 0] * vel[0, spans[side]] + patch[side, 1, 0] * vel[1, spans[side]]
        grad[spans[side]] = -filled(ice, (8, cols)) * product
        gradients[side].start()
    wait_all(gradients)
    for side in range(2):
        result(side).wait()


def whole(space=pltpu.VMEM):
    return pl.BlockSpec(memory_space=space)


def per_device(velocity, viscosity, friction, ice_mask, obs_tiles, obs_cell, obs_count):
    layers, rows, cols = viscosity.shape
    owners_x, owners_y, slots, channels, lanes = obs_tiles.shape[2:]
    blocks = cols // lanes
    tiles = blocks + 1
    owners = owners_x * owners_y
    steps = rows // 8
    f32 = jnp.float32

    def shape(*dims):
        return jax.ShapeDtypeStruct(dims, f32)

    def grant(mib):
        return pltpu.CompilerParams(vmem_limit_bytes=int(mib * MIB))

    def swap(value, axis, first):
        pairs = []
        for i in range(first, lax.axis_size(axis) - 1, 2):
            pairs += [(i, i + 1), (i + 1, i)]
        return lax.ppermute(value, axis, pairs)

    tiles_in = jnp.transpose(obs_tiles.reshape(owners, slots, channels, lanes), (0, 2, 1, 3))
    cells_in = jnp.transpose(obs_cell[0, 0], (1, 2, 0))
    counts_in = jnp.transpose(obs_count[0, 0], (1, 0))
    def part(dims, *index):
        return pl.BlockSpec(dims, lambda i: index)

    i32 = jnp.int32
    plane = shape(rows, lanes)
    hbm = whole(pltpu.HBM)
    anywhere = whole(pl.ANY)
    packed = pl.pallas_call(
        pack_kernel,
        out_shape=shape(owners, 4 * slots, lanes),
        in_specs=[hbm] * 3,
        out_specs=whole(),
        scratch_shapes=[
            pltpu.VMEM(counts_in.shape, i32),
            pltpu.VMEM(tiles_in.shape, f32),
            pltpu.VMEM(cells_in.shape, i32),
            pltpu.SemaphoreType.DMA((3,)),
        ],
        compiler_params=grant(61.5),
        cost_estimate=pl.CostEstimate(flops=4 * 10**9, transcendentals=0, bytes_accessed=0),
        name="pack",
    )(counts_in, tiles_in, cells_in)
    top = velocity[:, layers - 1]
    arrived = lax.all_to_all(packed, ("gx", "gy"), split_axis=0, concat_axis=0, tiled=True)
    ysend_one, ysend_two = pl.pallas_call(
        columns_kernel,
        out_shape=(plane, plane),
        in_specs=[hbm, whole(), whole(), whole()],
        out_specs=(whole(), whole()),
        scratch_shapes=[pltpu.VMEM((1, 1), i32), pltpu.SemaphoreType.DMA(())],
        compiler_params=grant(52),
        cost_estimate=pl.CostEstimate(flops=4 * 10**9, transcendentals=0, bytes_accessed=0),
        name="columns",
    )(ice_mask, viscosity, friction, top)
    yone = swap(ysend_one, "gy", 0)
    ytwo = swap(ysend_two, "gy", 1)

    own = shape(layers + 2, tiles, 8, lanes)
    edge = shape(layers + 4, tiles, 4, lanes)
    rhs, field, own_low, own_high, xsend_one, xsend_two = pl.pallas_call(
        functools.partial(sources_kernel, slots),
        out_shape=(
            shape(2, tiles, rows, lanes),
            shape(layers + 2, tiles, rows + 2 * MARGIN, lanes),
            own,
            own,
            edge,
            edge,
        ),
        in_specs=[hbm, whole(), hbm, hbm, whole(), whole(), whole()],
        out_specs=(whole(),) * 6,
        scratch_shapes=[
            pltpu.VMEM((1, 1), i32),
            pltpu.SemaphoreType.DMA((2 * blocks + 1,)),
        ],
        compiler_params=grant(47.5),
        cost_estimate=pl.CostEstimate(flops=4 * 10**9, transcendentals=0, bytes_accessed=0),
        name="sources",
    )(
        ice_mask, arrived.reshape(owners * 4 * slots, lanes), viscosity, friction, top, yone, ytwo
    )
    xone = swap(xsend_one, "gx", 0)
    xtwo = swap(xsend_two, "gx", 1)

    ends = shape(2, layers, blocks, 8, lanes)
    wide = pltpu.VMEM((2, layers, tiles, steps + 2, 8, lanes), f32)
    adjoint, low, high, base = pl.pallas_call(
        inner_kernel,
        out_shape=(shape(*velocity.shape), ends, ends, shape(2, rows, cols)),
        in_specs=[whole(), whole()],
        out_specs=(hbm, whole(), whole(), whole()),
        scratch_shapes=[
            pltpu.VMEM((steps, tiles, FACES, layers, 8, lanes), f32),
            wide,
            wide,
            pltpu.VMEM((2, layers, blocks, rows, lanes), f32),
            pltpu.SemaphoreType.DMA((blocks,)),
        ],
        compiler_params=grant(28),
        cost_estimate=pl.CostEstimate(flops=4 * 10**9, transcendentals=0, bytes_accessed=0),
        name="inner",
    )(field, rhs)

    return pl.pallas_call(
        edges_kernel,
        out_shape=(shape(*velocity.shape), shape(rows, cols)),
        in_specs=[hbm] + [whole()] * 8 + [hbm, hbm],
        out_specs=(hbm, hbm),
        scratch_shapes=[
            pltpu.VMEM((1, 1), i32),
            pltpu.VMEM((2, layers + 2, tiles, 16, lanes), f32),
            pltpu.VMEM((2, tiles, FACES, layers, 16, lanes), f32),
            pltpu.VMEM((2, 2, tiles, 16, lanes), f32),
            pltpu.VMEM((2, 2, layers, tiles, 16, lanes), f32),
            pltpu.VMEM((2, 2, layers, tiles, 16, lanes), f32),
            pltpu.VMEM((2, 2, layers, 8, cols), f32),
            pltpu.VMEM((2, rows, cols), f32),
            pltpu.VMEM((rows, cols), f32),
            pltpu.SemaphoreType.DMA((2,)),
            pltpu.SemaphoreType.DMA((5,)),
        ],
        input_output_aliases={10: 0},
        compiler_params=grant(14),
        cost_estimate=pl.CostEstimate(flops=4 * 10**9, transcendentals=0, bytes_accessed=0),
        name="edges",
    )(ice_mask, own_low, own_high, xone, xtwo, rhs, low, high, base, velocity, adjoint)


def solution(mesh):
    placed = (
        P(None, None, "gx", "gy"),
        P(None, "gx", "gy"),
        P("gx", "gy"),
        P("gx", "gy"),
        P("gx", "gy", None, None, None, None, None),
        P("gx", "gy", None, None, None),
        P("gx", "gy", None, None),
    )
    return jax.shard_map(
        per_device,
        mesh=mesh,
        in_specs=placed,
        out_specs=(P(None, None, "gx", "gy"), P("gx", "gy")),
        check_vma=False,
    )
```

```python
import functools

import jax
import jax.numpy as jnp
from jax import lax
from jax.experimental import pallas as pl
from jax.experimental.pallas import tpu as pltpu
from jax.sharding import PartitionSpec as P

VERTICAL_GAIN = 2.0
RELAX_WEIGHT = 0.8

MARGIN = 8
FACES = 6
MIB = 2**20


def lanes_of(shape):
    return lax.broadcasted_iota(jnp.int32, shape, len(shape) - 1)


def three_parts(value):
    high = value.astype(jnp.bfloat16)
    rest = value - high.astype(jnp.float32)
    middle = rest.astype(jnp.bfloat16)
    low = (rest - middle.astype(jnp.float32)).astype(jnp.bfloat16)
    return jnp.concatenate([high, middle, low], axis=-1)


def sum_parts(value):
    width = value.shape[-1] // 3
    return value[:, :width] + value[:, width : 2 * width] + value[:, 2 * width :]


def pick(onehot, value):
    return sum_parts(jnp.dot(onehot, three_parts(value), preferred_element_type=jnp.float32))


def spread(onehot, value):
    dims = (((0,), (0,)), ((), ()))
    return sum_parts(
        lax.dot_general(onehot, three_parts(value), dims, preferred_element_type=jnp.float32)
    )


def filled(ref, shape):
    return jnp.broadcast_to(ref[...], shape).astype(jnp.float32)


def is_even(axis):
    return lax.rem(lax.axis_index(axis), 2) == 0


def received(axis, one, two):
    even = is_even(axis)
    return jnp.where(even, two, one), jnp.where(even, one, two)


def fetch_all(copies):
    for copy in copies:
        copy.start()


def wait_all(copies):
    for copy in copies:
        copy.wait()


def pack_kernel(count_hbm, tiles_hbm, cells_hbm, out_ref, counts, tiles, cells, sems):
    owners_y, owners_x = counts.shape
    slots, lanes = tiles.shape[2], tiles.shape[3]
    pairs = [(count_hbm, counts), (cells_hbm, cells), (tiles_hbm, tiles)]
    copies = [pltpu.make_async_copy(a, b, sems.at[n]) for n, (a, b) in enumerate(pairs)]
    fetch_all(copies)
    wait_all(copies)
    lane = lanes_of((slots, lanes))
    slot = lax.broadcasted_iota(jnp.int32, (slots, lanes), 0)
    zero = jnp.zeros((slots, lanes), jnp.float32)
    for ox in range(owners_x):
        firsts, lasts, owns = [], [], []
        for oy in range(owners_y):
            owner = ox * owners_y + oy
            u = tiles[owner, 0]
            v = tiles[owner, 1]
            count = jnp.broadcast_to(counts[oy : oy + 1, ox : ox + 1], (slots, lanes))
            w = jnp.where(slot < count, tiles[owner, 2], 0.0)
            cell = jnp.broadcast_to(cells[oy, :, ox : ox + 1], (slots, lanes)).astype(jnp.float32)
            out_ref[owner, 0:slots] = u
            out_ref[owner, slots : 2 * slots] = v
            out_ref[owner, 2 * slots : 3 * slots] = w
            first = jnp.where(lane < 4, pltpu.roll(v, 2, 1), jnp.where(lane < 6, pltpu.roll(w, 4, 1), cell))
            firsts.append(jnp.where(lane < 2, u, first))
            last = jnp.where(
                lane >= lanes - 4,
                pltpu.roll(v, lanes - 2, 1),
                jnp.where(lane >= lanes - 6, pltpu.roll(w, lanes - 4, 1), cell),
            )
            lasts.append(jnp.where(lane >= lanes - 2, u, last))
            owns.append(cell)
        for oy in range(owners_y):
            after = firsts[oy + 1] if oy + 1 < owners_y else zero
            before = lasts[oy - 1] if oy > 0 else zero
            meta = jnp.where(lane < 16, after, jnp.where(lane >= lanes - 16, before, owns[oy]))
            out_ref[ox * owners_y + oy, 3 * slots : 4 * slots] = meta


def columns_kernel(ice_hbm, visc_ref, fric_ref, top_ref, one_ref, two_ref, ice, sem):
    layers, rows, cols = visc_ref.shape
    lanes = one_ref.shape[1]
    copy = pltpu.make_async_copy(ice_hbm, ice, sem)
    copy.start()
    copy.wait()
    left, right = slice(0, lanes), slice(cols - lanes, cols)
    lane = lanes_of((rows, lanes))
    icefield = filled(ice, (rows, lanes))
    first = jnp.zeros((rows, lanes), jnp.float32)
    last = jnp.zeros((rows, lanes), jnp.float32)
    for k in range(layers + 4):
        if k < layers:
            mine = (visc_ref[k, :, left], visc_ref[k, :, right])
        elif k == layers:
            mine = (fric_ref[:, left], fric_ref[:, right])
        elif k == layers + 1:
            mine = (icefield, icefield)
        else:
            mine = (top_ref[k - layers - 2, :, left], top_ref[k - layers - 2, :, right])
        here = (lane >= 3 * k) & (lane < 3 * k + 3)
        first = jnp.where(here, pltpu.roll(mine[0], 3 * k, 1), first)
        there = (lane >= lanes - 3 - 3 * k) & (lane < lanes - 3 * k)
        last = jnp.where(there, pltpu.roll(mine[1], (lanes - 3 * k) % lanes, 1), last)
    even = is_even("gy")
    one_ref[...] = jnp.where(even, last, first)
    two_ref[...] = jnp.where(even, first, last)


def side_tile(before, after, k):
    lanes = before.shape[-1]
    lane = lanes_of(before.shape)
    left = pltpu.roll(before, (3 * k) % lanes, 1)
    right = pltpu.roll(after, (lanes - 3 * k) % lanes, 1)
    return jnp.where(lane < 3, right, jnp.where(lane >= lanes - 3, left, 0.0))


def ring_pair(load, tile, tiles):
    here = load(tile)
    lanes = here.shape[-1]
    lane = lanes_of(here.shape)
    before = pltpu.roll(jnp.where(lane == lanes - 1, load((tile - 1) % tiles), here), 1, 1)
    after = pltpu.roll(jnp.where(lane == 0, load((tile + 1) % tiles), here), lanes - 1, 1)
    return here, before, after


def factor_columns(layers, tile, tiles, load, store):
    gain = (0.5 * RELAX_WEIGHT) * load(layers + 1, tile, 0)
    up = None
    ratio = None
    for k in range(layers):
        here, south, north = ring_pair(lambda s: load(k, s, 0), tile, tiles)
        west = here + load(k, tile, -1)
        east = here + load(k, tile, 1)
        south = here + south
        north = here + north
        entry = 0.5 * (west + east + south + north)
        if k == 0:
            entry = entry + load(layers, tile, 0)
        if k > 0:
            entry = entry + (up - up * ratio)
        if k < layers - 1:
            above = (0.5 * VERTICAL_GAIN) * (here + load(k + 1, tile, 0))
            entry = entry + above
        inverse = jnp.where(entry > 0.0, 1.0 / entry, 0.0)
        scale = gain * inverse
        store(0, k, west * scale)
        store(1, k, east * scale)
        store(2, k, south * scale)
        store(3, k, north * scale)
        if k > 0:
            store(4, k, up * inverse)
        if k < layers - 1:
            up = above
            ratio = up * inverse
            store(5, k, ratio)
        else:
            store(4, 0, 2.0 * scale)


def first_columns(layers, rhs, coef, store):
    for n in range(2):
        value = rhs(n) * coef(4, 0)
        store(n, layers - 1, value)
        for k in range(layers - 2, -1, -1):
            value = coef(5, k) * value
            store(n, k, value)


def relax_columns(layers, tile, tiles, old, rhs, coef, store):
    forward = [[], []]
    for k in range(layers):
        west, east, south, north = (coef(f, k) for f in range(4))
        for n in range(2):
            here, before, after = ring_pair(lambda s: old(n, k, s, 0), tile, tiles)
            value = west * old(n, k, tile, -1) + east * old(n, k, tile, 1)
            value = value + (south * before + north * after)
            if k > 0:
                value = value + coef(4, k) * forward[n][k - 1]
            if k == layers - 1:
                value = value + rhs(n) * coef(4, 0)
            forward[n].append(value)
    for n in range(2):
        value = forward[n][layers - 1]
        for k in range(layers - 1, -1, -1):
            if k < layers - 1:
                value = forward[n][k] + coef(5, k) * value
            store(n, k, (1.0 - RELAX_WEIGHT) * old(n, k, tile, 0) + value)


def sources_kernel(
    slots, ice_hbm, tiles_ref, visc_hbm, fric_hbm, vel, one, two,
    rhs_ref, field, low_ref, high_ref, xone_ref, xtwo_ref, ice, sems,
):
    layers, rows, cols = visc_hbm.shape
    lanes = tiles_ref.shape[1]
    owners = tiles_ref.shape[0] // (4 * slots)
    blocks = cols // lanes
    middle = pl.ds(MARGIN, rows)
    pairs = [(ice_hbm, ice)]
    for t in range(blocks):
        span = pl.ds(t * lanes, lanes)
        pairs.append((visc_hbm.at[:, :, span], field.at[pl.ds(0, layers), t, middle, :]))
        pairs.append((fric_hbm.at[:, span], field.at[layers, t, middle, :]))
    copies = [pltpu.make_async_copy(a, b, sems.at[n]) for n, (a, b) in enumerate(pairs)]
    fetch_all(copies)
    edge = jnp.zeros((MARGIN, lanes), jnp.float32)
    for k in range(layers):
        for t in range(blocks + 1):
            field[k, t, 0:MARGIN] = edge
            field[k, t, MARGIN + rows : 2 * MARGIN + rows] = edge

    def channel(c):
        return jnp.concatenate(
            [tiles_ref[pl.ds(c * slots + s, owners, stride=4 * slots), :] for s in range(slots)], axis=0
        )

    seen_u, seen_v, weight, meta = channel(0), channel(1), channel(2), channel(3)
    count = owners * slots
    lane = lanes_of((count, lanes))
    row = lanes_of((count, rows))

    def onehot(column, b):
        cell = jnp.broadcast_to(column.astype(jnp.int32), (count, rows))
        return (cell == row * blocks + b).astype(jnp.bfloat16)

    even = is_even("gx")

    def send(k, t, low, high):
        xone_ref[k, t] = jnp.where(even, high, low)
        xtwo_ref[k, t] = jnp.where(even, low, high)

    def put(c, t, plane):
        rhs_ref[c, t] = plane
        send(layers + 2 + c, t, plane[0:4], plane[rows - 4 : rows])

    own = meta[:, lanes // 2 : lanes // 2 + 1]
    marks = jnp.concatenate([onehot(own, b) for b in range(blocks)], axis=1)
    surface = jnp.concatenate(
        [
            jnp.concatenate([vel[c, :, b * lanes : (b + 1) * lanes] for b in range(blocks)], axis=0)
            for c in range(2)
        ],
        axis=1,
    )
    weights = jnp.concatenate([weight, weight], axis=1)
    terms = weights * (pick(marks, surface) - jnp.concatenate([seen_u, seen_v], axis=1))
    total = spread(marks, terms)
    for c in range(2):
        for b in range(blocks):
            put(c, b, total[b * rows : (b + 1) * rows, c * lanes : (c + 1) * lanes])

    wait_all(copies[:1])
    icefield = filled(ice, (rows, lanes))
    from_before, from_after = received("gy", one[...], two[...])
    for k in range(layers + 2):
        field[k, blocks, middle] = side_tile(from_before, from_after, k)
        for t in range(blocks):
            if k == layers + 1:
                field[k, t, middle] = icefield
    beside = jnp.concatenate(
        [side_tile(from_before, from_after, layers + 2 + c) for c in range(2)], axis=1
    )
    mark_after = onehot(meta[:, 8:9], 0)
    mark_before = onehot(meta[:, lanes - 8 : lanes - 7], blocks - 1)
    weight_after = jnp.where(lane < 2, pltpu.roll(meta, lanes - 4, 1), 0.0)
    weight_before = jnp.where(lane >= lanes - 2, pltpu.roll(meta, 4, 1), 0.0)
    after = jnp.concatenate([meta, pltpu.roll(meta, lanes - 2, 1)], axis=1)
    before = jnp.concatenate([meta, pltpu.roll(meta, 2, 1)], axis=1)
    terms_after = jnp.concatenate([weight_after] * 2, axis=1) * (pick(mark_after, beside) - after)
    terms_before = jnp.concatenate([weight_before] * 2, axis=1) * (pick(mark_before, beside) - before)
    side = spread(mark_after, terms_after) + spread(mark_before, terms_before)
    for c in range(2):
        put(c, blocks, side[:, c * lanes : (c + 1) * lanes])

    wait_all(copies[1:])
    for k in range(layers + 2):
        for t in range(blocks + 1):
            low = field[k, t, MARGIN : MARGIN + 8]
            high = field[k, t, MARGIN + rows - 8 : MARGIN + rows]
            low_ref[k, t] = low
            high_ref[k, t] = high
            send(k, t, low[0:4], high[4:8])


def inner_kernel(field, rhs, adj_hbm, low_ref, high_ref, base_ref, last_ref, coef, one, two, three, sem_out):
    steps, tiles, _, layers, _, lanes = coef.shape
    rows = last_ref.shape[2]
    def factors(r, carry):
        for t in range(tiles):

            def load(k, s, move):
                return field[k, s, pl.ds(MARGIN + r + move, 8, stride=steps), :]

            def store(f, k, value):
                coef[r, t, f, k] = value

            factor_columns(layers, t, tiles, load, store)
        return carry

    lax.fori_loop(0, steps, factors, 0, unroll=6)

    sublane = lax.broadcasted_iota(jnp.int32, (8, lanes), 0)

    def wrap(ref):
        for n in range(2):
            for k in range(layers):
                for t in range(tiles):
                    last = pltpu.roll(ref[n, k, t, steps], 1, 0)
                    ref[n, k, t, 0] = jnp.where(sublane == 0, 0.0, last)
                    first = pltpu.roll(ref[n, k, t, 1], 7, 0)
                    ref[n, k, t, steps + 1] = jnp.where(sublane == 7, 0.0, first)

    def rhs_of(r, t):
        return lambda n: rhs[n, t, pl.ds(r, 8, stride=steps), :]

    def coef_of(r, t):
        return lambda f, k: coef[r, t, f, k]

    def first_sweep(r, carry):
        for t in range(tiles):

            def store(n, k, value):
                one[n, k, t, r + 1] = value

            first_columns(layers, rhs_of(r, t), coef_of(r, t), store)
        return carry

    lax.fori_loop(0, steps, first_sweep, 0, unroll=6)
    wrap(one)

    def second_sweep(r, carry):
        for t in range(tiles):

            def old(n, k, s, move):
                return one[n, k, s, r + 1 + move]

            def store(n, k, value):
                two[n, k, t, r + 1] = value

            relax_columns(layers, t, tiles, old, rhs_of(r, t), coef_of(r, t), store)
        return carry

    lax.fori_loop(0, steps, second_sweep, 0, unroll=4)
    wrap(two)

    def result(t):
        middle = pl.ds(8, rows - 16)
        span = pl.ds(t * lanes, lanes)
        return pltpu.make_async_copy(three.at[:, :, t, middle, :], adj_hbm.at[:, :, middle, span], sem_out.at[t])

    for t in range(tiles - 1):
        found = last_ref if t == tiles - 2 else three.at[:, :, t]

        def third_sweep(r, carry):
            def old(n, k, s, move):
                return two[n, k, s, r + 1 + move]

            def store(n, k, value):
                found[n, k, pl.ds(r, 8, stride=steps), :] = value

            relax_columns(layers, t, tiles, old, rhs_of(r, t), coef_of(r, t), store)
            return carry

        lax.fori_loop(0, steps, third_sweep, 0, unroll=12)
        if t < tiles - 2:
            result(t).start()
        for n in range(2):
            for k in range(layers):
                low_ref[n, k, t] = found[n, k, 0:8]
                high_ref[n, k, t] = found[n, k, rows - 8 : rows]
        for n in range(2):
            base_ref[n, :, t * lanes : (t + 1) * lanes] = found[n, 0]
    for t in range(tiles - 2):
        result(t).wait()


def edges_kernel(
    ice_hbm, own_low, own_high, one_ref, two_ref, rhs_ref, low_ref, high_ref, base_ref, last_ref, vel_hbm, adj_in,
    adj_hbm, grad_hbm, ice, field, coefs, rhs, one, two, patch, vel, grad, sem_in, sem_out,
):
    tiles, _, layers = coefs.shape[1:4]
    rows, cols = grad.shape
    lanes = coefs.shape[5]
    blocks = tiles - 1
    spans = [pl.ds(0, 8), pl.ds(rows - 8, 8), pl.ds(8, rows - 16)]
    gradients = [
        pltpu.make_async_copy(grad.at[span, :], grad_hbm.at[span, :], sem_out.at[2 + n])
        for n, span in enumerate(spans)
    ]
    fetches = [
        pltpu.make_async_copy(vel_hbm.at[:, 0], vel, sem_in.at[0]),
        pltpu.make_async_copy(ice_hbm, ice, sem_in.at[1]),
    ]
    fetch_all(fetches)
    inside = spans[2]
    rest = pltpu.make_async_copy(
        last_ref.at[:, :, inside, :], adj_hbm.at[:, :, inside, pl.ds(cols - lanes, lanes)], sem_out.at[5]
    )
    rest.start()
    for k in range(layers + 4):
        for t in range(tiles):
            before, after = received("gx", one_ref[k, t], two_ref[k, t])
            if k < layers + 2:
                field[0, k, t, 0:4] = before
                field[0, k, t, 4:12] = own_low[k, t]
                field[1, k, t, 4:12] = own_high[k, t]
                field[1, k, t, 12:16] = after
            else:
                n = k - layers - 2
                rhs[0, n, t, 0:4] = before
                rhs[0, n, t, 4:12] = rhs_ref[n, t, 0:8]
                rhs[1, n, t, 4:12] = rhs_ref[n, t, rows - 8 : rows]
                rhs[1, n, t, 12:16] = after
    starts = (2, 6)

    def at(ref, start):
        return lambda *index: ref[(*index, pl.ds(start, 8), slice(None))]

    for t in range(tiles):
        for side in range(2):

            def load(k, s, move):
                return field[side, k, s, pl.ds(starts[side] + move, 8), :]

            def store(f, k, value):
                coefs[side, t, f, k, pl.ds(starts[side], 8), :] = value

            factor_columns(layers, t, tiles, load, store)

    def sides(t, start, side):
        def rhs_of(n):
            return rhs[side, n, t, pl.ds(start, 8), :]

        def coef(f, k):
            return coefs[side, t, f, k, pl.ds(start, 8), :]

        return rhs_of, coef

    for t in range(tiles):
        for side in range(2):
            rhs_of, coef = sides(t, starts[side], side)

            def store(n, k, value):
                one[side, n, k, t, pl.ds(starts[side], 8), :] = value

            first_columns(layers, rhs_of, coef, store)
    for t in range(tiles):
        for side in range(2):
            rhs_of, coef = sides(t, starts[side], side)

            def old(n, k, s, move):
                return one[side, n, k, s, pl.ds(starts[side] + move, 8), :]

            def store(n, k, value):
                two[side, n, k, t, pl.ds(starts[side], 8), :] = value

            relax_columns(layers, t, tiles, old, rhs_of, coef, store)

    wait_all(fetches)
    product = base_ref[0, inside] * vel[0, inside] + base_ref[1, inside] * vel[1, inside]
    grad[inside] = -filled(ice, (rows - 16, cols)) * product
    gradients[2].start()

    def result(side):
        return pltpu.make_async_copy(
            patch.at[side], adj_hbm.at[:, :, pl.ds(side * (rows - 8), 8), :], sem_out.at[side]
        )

    sublane = lax.broadcasted_iota(jnp.int32, (8, lanes), 0)
    wrong = (sublane < 3, sublane >= 5)
    inner = (low_ref, high_ref)
    for side in range(2):
        for t in range(blocks):
            rhs_of, coef = sides(t, 4, side)
            span = slice(t * lanes, (t + 1) * lanes)

            def old(n, k, s, move):
                return two[side, n, k, s, pl.ds(4 + move, 8), :]

            def store(n, k, value):
                patch[side, n, k, :, span] = jnp.where(wrong[side], value, inner[side][n, k, t])

            relax_columns(layers, t, tiles, old, rhs_of, coef, store)
        result(side).start()
    for side in range(2):
        product = patch[side, 0, 0] * vel[0, spans[side]] + patch[side, 1, 0] * vel[1, spans[side]]
        grad[spans[side]] = -filled(ice, (8, cols)) * product
        gradients[side].start()
    wait_all(gradients)
    rest.wait()
    for side in range(2):
        result(side).wait()


def whole(space=pltpu.VMEM):
    return pl.BlockSpec(memory_space=space)


def per_device(velocity, viscosity, friction, ice_mask, obs_tiles, obs_cell, obs_count):
    layers, rows, cols = viscosity.shape
    owners_x, owners_y, slots, channels, lanes = obs_tiles.shape[2:]
    blocks = cols // lanes
    tiles = blocks + 1
    owners = owners_x * owners_y
    steps = rows // 8
    f32 = jnp.float32

    def shape(*dims):
        return jax.ShapeDtypeStruct(dims, f32)

    def grant(mib):
        return pltpu.CompilerParams(vmem_limit_bytes=int(mib * MIB))

    def swap(value, axis, first):
        pairs = []
        for i in range(first, lax.axis_size(axis) - 1, 2):
            pairs += [(i, i + 1), (i + 1, i)]
        return lax.ppermute(value, axis, pairs)

    tiles_in = jnp.transpose(obs_tiles.reshape(owners, slots, channels, lanes), (0, 2, 1, 3))
    cells_in = jnp.transpose(obs_cell[0, 0], (1, 2, 0))
    counts_in = jnp.transpose(obs_count[0, 0], (1, 0))
    def part(dims, *index):
        return pl.BlockSpec(dims, lambda i: index)

    i32 = jnp.int32
    plane = shape(rows, lanes)
    hbm = whole(pltpu.HBM)
    anywhere = whole(pl.ANY)
    packed = pl.pallas_call(
        pack_kernel,
        out_shape=shape(owners, 4 * slots, lanes),
        in_specs=[hbm] * 3,
        out_specs=whole(),
        scratch_shapes=[
            pltpu.VMEM(counts_in.shape, i32),
            pltpu.VMEM(tiles_in.shape, f32),
            pltpu.VMEM(cells_in.shape, i32),
            pltpu.SemaphoreType.DMA((3,)),
        ],
        compiler_params=grant(61.5),
        cost_estimate=pl.CostEstimate(flops=4 * 10**9, transcendentals=0, bytes_accessed=0),
        name="pack",
    )(counts_in, tiles_in, cells_in)
    top = velocity[:, layers - 1]
    arrived = lax.all_to_all(packed, ("gx", "gy"), split_axis=0, concat_axis=0, tiled=True)
    ysend_one, ysend_two = pl.pallas_call(
        columns_kernel,
        out_shape=(plane, plane),
        in_specs=[hbm, whole(), whole(), whole()],
        out_specs=(whole(), whole()),
        scratch_shapes=[pltpu.VMEM((1, 1), i32), pltpu.SemaphoreType.DMA(())],
        compiler_params=grant(52),
        cost_estimate=pl.CostEstimate(flops=4 * 10**9, transcendentals=0, bytes_accessed=0),
        name="columns",
    )(ice_mask, viscosity, friction, top)
    yone = swap(ysend_one, "gy", 0)
    ytwo = swap(ysend_two, "gy", 1)

    own = shape(layers + 2, tiles, 8, lanes)
    edge = shape(layers + 4, tiles, 4, lanes)
    rhs, field, own_low, own_high, xsend_one, xsend_two = pl.pallas_call(
        functools.partial(sources_kernel, slots),
        out_shape=(
            shape(2, tiles, rows, lanes),
            shape(layers + 2, tiles, rows + 2 * MARGIN, lanes),
            own,
            own,
            edge,
            edge,
        ),
        in_specs=[hbm, whole(), hbm, hbm, whole(), whole(), whole()],
        out_specs=(whole(),) * 6,
        scratch_shapes=[
            pltpu.VMEM((1, 1), i32),
            pltpu.SemaphoreType.DMA((2 * blocks + 1,)),
        ],
        compiler_params=grant(47.5),
        cost_estimate=pl.CostEstimate(flops=4 * 10**9, transcendentals=0, bytes_accessed=0),
        name="sources",
    )(
        ice_mask, arrived.reshape(owners * 4 * slots, lanes), viscosity, friction, top, yone, ytwo
    )
    xone = swap(xsend_one, "gx", 0)
    xtwo = swap(xsend_two, "gx", 1)

    ends = shape(2, layers, blocks, 8, lanes)
    wide = pltpu.VMEM((2, layers, tiles, steps + 2, 8, lanes), f32)
    adjoint, low, high, base, last = pl.pallas_call(
        inner_kernel,
        out_shape=(shape(*velocity.shape), ends, ends, shape(2, rows, cols), shape(2, layers, rows, lanes)),
        in_specs=[whole(), whole()],
        out_specs=(hbm, whole(), whole(), whole(), whole()),
        scratch_shapes=[
            pltpu.VMEM((steps, tiles, FACES, layers, 8, lanes), f32),
            wide,
            wide,
            pltpu.VMEM((2, layers, blocks - 1, rows, lanes), f32),
            pltpu.SemaphoreType.DMA((blocks - 1,)),
        ],
        compiler_params=grant(28),
        cost_estimate=pl.CostEstimate(flops=4 * 10**9, transcendentals=0, bytes_accessed=0),
        name="inner",
    )(field, rhs)

    return pl.pallas_call(
        edges_kernel,
        out_shape=(shape(*velocity.shape), shape(rows, cols)),
        in_specs=[hbm] + [whole()] * 9 + [hbm, hbm],
        out_specs=(hbm, hbm),
        scratch_shapes=[
            pltpu.VMEM((1, 1), i32),
            pltpu.VMEM((2, layers + 2, tiles, 16, lanes), f32),
            pltpu.VMEM((2, tiles, FACES, layers, 16, lanes), f32),
            pltpu.VMEM((2, 2, tiles, 16, lanes), f32),
            pltpu.VMEM((2, 2, layers, tiles, 16, lanes), f32),
            pltpu.VMEM((2, 2, layers, tiles, 16, lanes), f32),
            pltpu.VMEM((2, 2, layers, 8, cols), f32),
            pltpu.VMEM((2, rows, cols), f32),
            pltpu.VMEM((rows, cols), f32),
            pltpu.SemaphoreType.DMA((2,)),
            pltpu.SemaphoreType.DMA((6,)),
        ],
        input_output_aliases={11: 0},
        compiler_params=grant(14),
        cost_estimate=pl.CostEstimate(flops=4 * 10**9, transcendentals=0, bytes_accessed=0),
        name="edges",
    )(ice_mask, own_low, own_high, xone, xtwo, rhs, low, high, base, last, velocity, adjoint)


def solution(mesh):
    placed = (
        P(None, None, "gx", "gy"),
        P(None, "gx", "gy"),
        P("gx", "gy"),
        P("gx", "gy"),
        P("gx", "gy", None, None, None, None, None),
        P("gx", "gy", None, None, None),
        P("gx", "gy", None, None),
    )
    return jax.shard_map(
        per_device,
        mesh=mesh,
        in_specs=placed,
        out_specs=(P(None, None, "gx", "gy"), P("gx", "gy")),
        check_vma=False,
    )
```
